32 devices in a mesh: ctx: 8 (over y, x, core), seq: 4 (over z).
Axes of the slice: x: 2, y: 2, z: 4, core: 2. Of those that a mesh axis runs over, the one named last changes fastest.
Arguments:
- queries: bfloat16 [4096, 4096], P(('seq', 'ctx')), may hold values from -6 to 6
- key_proj: bfloat16 [4096, 4096], P(('seq', 'ctx')), may hold values from -6 to 6
- value_proj: bfloat16 [4096, 4096], P(('seq', 'ctx')), may hold values from -6 to 6
- decay_rate: float32 [16, 4096], P(None, 'ctx'), may hold values from 2.4414063e-05 to 0.06
- residue: float32 [16, 4096], P(None, 'ctx'), may hold values from -1 to 1
- skip_gain: float32 [4096], P('ctx'), may hold values from -1 to 1
Outputs:
- operator_out: bfloat16 [4096, 4096], P(('seq', 'ctx'))
The draws below stay inside these ranges and needn't reach their ends.
All inputs are finite; a program needn't handle non-finite values.
Results may differ from the reference program's by a relative error of at most 0.011.
Values may be sent and summed in bfloat16 or wider, within the bound.
A program may use at most 320 MiB of HBM per device.

```python
import math
import jax
import jax.numpy as jnp
from jax import lax

D = 4096
MODES = 16
LENGTH = 4096
N_CTX = 8


def draw_decay_rate(key, part):
    pick_key, slow_key, fast_key = jax.random.split(key, 3)
    shape = (MODES, D)
    slow_low = math.log(0.1 / LENGTH)
    slow_high = math.log(2.3 / LENGTH)
    fast_high = math.log(0.06)
    share = 0.5
    slow_rates = jnp.exp(jax.random.uniform(slow_key, shape, jnp.float32, slow_low, slow_high))
    fast_rates = jnp.exp(jax.random.uniform(fast_key, shape, jnp.float32, slow_high, fast_high))
    chosen = jax.random.uniform(pick_key, shape, jnp.float32) < share
    return jnp.where(chosen, slow_rates, fast_rates).astype(jnp.float32)


def steps_of(key, shape, cuts, smallest, top_value):
    factor_of, own = 1.0, jax.random.fold_in(key, 6)
    for dim, parts in cuts:
        steps = jnp.exp(jax.random.uniform(jax.random.fold_in(own, dim), (parts,), jnp.float32, smallest / len(cuts), top_value / len(cuts)))
        factor_of = factor_of * jnp.repeat(steps, shape[dim] // parts).reshape([-1 if axis == dim else 1 for axis in range(len(shape))])
    return factor_of


def bell_draw(key, shape, width, reach, cuts=(), held_as=jnp.bfloat16):
    loudness = steps_of(key, shape, cuts, -0.22, 0.18) if cuts else 1.0
    entries = jax.random.normal(key, shape, jnp.float32) * width * loudness
    return jnp.minimum(jnp.maximum(entries, -reach), reach).astype(held_as)


def setup_inputs(seed: int = 0) -> dict:
    streams_of = jax.random.split(jax.random.key(seed), 7)
    return {
        "queries": bell_draw(streams_of[0], (LENGTH, D), 1.0, 6.0, ((0, 32),)),
        "key_proj": bell_draw(streams_of[1], (LENGTH, D), 1.0, 6.0, ((0, 32),)),
        "value_proj": bell_draw(streams_of[2], (LENGTH, D), 1.0, 6.0, ((0, 32),)),
        "decay_rate": draw_decay_rate(jax.random.fold_in(streams_of[6], 71), 0),
        "residue": bell_draw(streams_of[4], (MODES, D), 0.25, 1.0, ((1, 8),), jnp.float32),
        "skip_gain": jnp.clip(jax.random.uniform(streams_of[5], (D,), jnp.float32, -1.0, 1.0) * steps_of(streams_of[5], (D,), ((0, 8),), -0.4, 0.0), -1.0, 1.0),
    }


def link_states(earlier, later):
    return (later[1] * earlier[0] + later[0], earlier[1] * later[1])

def mode_tables(rate, resid, block_len):
    lag_steps = jnp.arange(block_len, dtype=jnp.float32)
    powers = jnp.exp(-rate[None, :, :] * lag_steps[:, None, None])
    weight = resid * jnp.sqrt(-jnp.expm1(-2.0 * rate))
    return (powers, weight)

def local_pass(signal, powers, weight, rate, block_len):
    length, columns = signal.shape
    nblocks = length // block_len
    kernel = jnp.einsum('jmc,mc->jc', powers, weight, precision=lax.Precision.HIGHEST)
    lag_grid = jnp.arange(block_len, dtype=jnp.int32)[:, None] - jnp.arange(block_len, dtype=jnp.int32)[None, :]
    toeplitz = jnp.where((lag_grid >= 0)[:, :, None], kernel[jnp.clip(lag_grid, 0, block_len - 1)], 0.0)
    blocks = signal.reshape(nblocks, block_len, columns)
    inner_part = jnp.einsum('tsc,bsc->btc', toeplitz, blocks, precision=lax.Precision.HIGHEST)
    block_ends = jnp.einsum('bsc,smc->bmc', blocks, powers[::-1], precision=lax.Precision.HIGHEST)
    block_decay = jnp.broadcast_to(jnp.exp(-rate * block_len)[None], block_ends.shape)
    run_states, run_decay = lax.associative_scan(link_states, (block_ends, block_decay), axis=0)
    before = jnp.concatenate([jnp.zeros_like(run_states[:1]), run_states[:-1]], axis=0)
    return (inner_part, before, run_states[-1])

def finish(inner_part, before, start_state, powers, weight, rate, block_len):
    nblocks = before.shape[0]
    block_starts = jnp.arange(nblocks, dtype=jnp.float32) * block_len
    offsets = jnp.exp(-rate[None, :, :] * block_starts[:, None, None])
    states = before + offsets * start_state[None]
    lift_table = powers * (jnp.exp(-rate) * weight)[None]
    carried = jnp.einsum('bmc,tmc->btc', states, lift_table, precision=lax.Precision.HIGHEST)
    return (inner_part + carried).reshape(nblocks * block_len, -1)

def reference(queries, key_proj, value_proj, decay_rate, residue, skip_gain):
    mixed_rows = (key_proj.astype(jnp.float32) * value_proj.astype(jnp.float32)).astype(jnp.bfloat16)
    length = queries.shape[0]
    columns = queries.shape[1]
    groups = N_CTX
    group_width = columns // groups
    block_len = math.gcd(length, 32)

    def split_cols(array):
        return array.reshape(array.shape[0], groups, group_width).transpose(1, 0, 2)

    def one_group(pieces):
        query_g, mixed_g, rate_g, resid_g, gain_g = pieces
        signal = mixed_g.astype(jnp.float32)
        powers, weight = mode_tables(rate_g, resid_g, block_len)
        inner_part, before, end_state = local_pass(signal, powers, weight, rate_g, block_len)
        filtered = finish(inner_part, before, jnp.zeros_like(end_state), powers, weight, rate_g, block_len)
        pre_gate = lax.optimization_barrier((filtered + gain_g[None, :] * signal).astype(jnp.bfloat16))
        return (query_g.astype(jnp.float32) * pre_gate.astype(jnp.float32)).astype(jnp.bfloat16)
    results = lax.map(one_group, (split_cols(queries), split_cols(mixed_rows), split_cols(decay_rate), split_cols(residue), skip_gain.reshape(groups, group_width)))
    return results.transpose(1, 0, 2).reshape(length, columns)
```

```python
import functools

import jax
import jax.numpy as jnp
from jax import lax
from jax.experimental import pallas as pl
from jax.experimental.pallas import tpu as pltpu
from jax.sharding import PartitionSpec as P

LANES = 128
BLOCKS = 8
MESH = pl.DeviceIdType.MESH


def kernel(
    nctx, nseq, modes, par_in, q_hbm, k_hbm, v_hbm, out_hbm,
    par, kbuf, vbuf, qbuf, obuf, mixed, inner, carry, pows, state_out, state_in, local_start,
    totals, start_out, start_in, turned,
    k_sem, v_sem, q_sem, o_sem, par_send, par_recv, st_send, st_recv, tot_send, tot_recv,
    go_send, go_recv,
):
    ctx, seq = lax.axis_index("ctx"), lax.axis_index("seq")
    tokens, width = kbuf.shape[1], kbuf.shape[2]
    groups = width // LANES
    steps = tokens // BLOCKS

    def slot(i):
        return lax.rem(ctx + i, nctx)

    def columns(c):
        return pl.ds(pl.multiple_of(c * width, LANES), width)

    def fetch(hbm, buf, sem, c):
        return pltpu.make_async_copy(hbm.at[:, columns(c)], buf.at[c], sem.at[c])

    def store_out(c):
        return pltpu.make_async_copy(obuf.at[c], out_hbm.at[:, columns(c)], o_sem.at[c])

    def swap(src, dst, to, send, recv, axis, other):
        return pltpu.make_async_remote_copy(
            src_ref=src, dst_ref=dst.at[to], send_sem=send.at[other], recv_sem=recv.at[to],
            device_id={axis: other}, device_id_type=MESH)

    def par_copy(c, to):
        return swap(par_in, par, to, par_send, par_recv, "ctx", c)

    def state_copy(c, to):
        return swap(state_out.at[c], state_in, to, st_send, st_recv, "ctx", c)

    def total_copy(s, to):
        return swap(totals.at[seq], totals, to, tot_send, tot_recv, "seq", s)

    def start_copy(c, to):
        return swap(start_out.at[c], start_in, to, go_send, go_recv, "ctx", c)

    def each(count, body):
        lax.fori_loop(0, count, lambda i, x: (body(i), x)[1], 0)

    @functools.partial(each, nctx)
    def _(i):
        fetch(k_hbm, kbuf, k_sem, slot(i)).start()
        fetch(v_hbm, vbuf, v_sem, slot(i)).start()

    barrier = pltpu.get_barrier_semaphore()

    @functools.partial(each, nctx - 1)
    def _(i):
        pl.semaphore_signal(barrier, inc=1, device_id={"ctx": slot(i + 1)}, device_id_type=MESH)

    @functools.partial(each, nseq - 1)
    def _(i):
        pl.semaphore_signal(
            barrier, inc=1, device_id={"seq": lax.rem(seq + i + 1, nseq)}, device_id_type=MESH)

    pl.semaphore_wait(barrier, nctx + nseq - 2)

    @functools.partial(each, nctx - 1)
    def _(i):
        par_copy(slot(i + 1), ctx).start()

    par[ctx] = par_in[...]

    @functools.partial(each, nctx)
    def _(i):
        fetch(q_hbm, qbuf, q_sem, slot(i)).start()

    block = lax.broadcasted_iota(jnp.int32, (BLOCKS, LANES), 0)

    def lanes(j):
        return pl.ds(pl.multiple_of(j * LANES, LANES), LANES)

    def wide(row):
        return jnp.broadcast_to(row, (BLOCKS, LANES))

    @functools.partial(each, nctx)
    def _(i):
        c = slot(i)

        @pl.when(i > 0)
        def _():
            par_copy(c, c).wait_recv()

        fetch(k_hbm, kbuf, k_sem, c).wait()
        fetch(v_hbm, vbuf, v_sem, c).wait()

        @functools.partial(each, groups)
        def _(j):
            g = c * groups + j
            product = kbuf[c, :, lanes(j)].astype(jnp.float32) * vbuf[c, :, lanes(j)].astype(jnp.float32)
            mixed[g] = product.astype(jnp.bfloat16).astype(jnp.float32)
            rate = par[c, 0:modes, lanes(j)]
            pows[g, 0:modes, :] = jnp.exp(-rate)
            pows[g, modes:2 * modes, :] = jnp.exp(-steps * rate)
            x = [mixed[g, pl.ds(a, BLOCKS, stride=steps), :] for a in range(steps)]
            for m in range(modes):
                p = wide(pows[g, pl.ds(m, 1), :])
                span = wide(pows[g, pl.ds(modes + m, 1), :])
                state = x[0]
                for a in range(1, steps):
                    state = state * p + x[a]
                shift = 1
                while shift < BLOCKS:
                    moved = pltpu.roll(state, shift, 0)
                    state = state + jnp.where(block >= shift, span, 0.0) * moved
                    span = span * span
                    shift *= 2
                carry[g, m] = jnp.where(block >= 1, pltpu.roll(state, 1, 0), 0.0)
                state_out[c, pl.ds(m, 1), lanes(j)] = state[BLOCKS - 1:, :]

        @pl.when(i > 0)
        def _():
            state_copy(c, ctx).start()

    def inside(first, last):
        def one(i):
            c = slot(i)

            @functools.partial(each, groups)
            def _(j):
                g = c * groups + j
                p = pows[g, 0:modes, :]
                w = par[c, modes:2 * modes, lanes(j)]
                gain = par[c, pl.ds(2 * modes, 1), lanes(j)]
                taps = []
                for a in range(steps):
                    tap = jnp.sum(w, axis=0, keepdims=True)
                    taps.append(wide(tap + gain if a == 0 else tap))
                    w = w * p
                x = [mixed[g, pl.ds(a, BLOCKS, stride=steps), :] for a in range(steps)]
                for a in range(steps):
                    y = taps[0] * x[a]
                    for b in range(a):
                        y = y + taps[a - b] * x[b]
                    inner[g, a] = y

        lax.fori_loop(first, last, lambda i, x: (one(i), x)[1], 0)

    cut = [0, (nctx * 3) // 8, (nctx * 6) // 8, nctx]
    inside(cut[0], cut[1])

    state_in[ctx] = state_out[ctx]

    @functools.partial(each, nctx - 1)
    def _(i):
        state_copy(slot(i + 1), slot(i + 1)).wait_recv()

    rate = par_in[0:modes, :]
    decay = jnp.exp(-tokens * rate)

    def link(s, state):
        local_start[s] = state
        return state * decay + state_in[s]

    totals[seq] = lax.fori_loop(0, nctx, link, jnp.zeros_like(rate))

    @functools.partial(each, nseq - 1)
    def _(i):
        total_copy(lax.rem(seq + i + 1, nseq), seq).start()

    inside(cut[1], cut[2])

    @functools.partial(each, nseq - 1)
    def _(i):
        s = lax.rem(seq + i + 1, nseq)
        total_copy(s, s).wait_recv()

    span_decay = jnp.exp(-(tokens * nctx) * rate)
    begin = lax.fori_loop(
        0, seq, lambda s, state: state * span_decay + totals[s], jnp.zeros_like(rate))

    @functools.partial(each, nctx)
    def _(i):
        c = slot(i)
        reach = jnp.exp(-(tokens * c).astype(jnp.float32) * rate)
        start_out[c] = local_start[c] + reach * begin

        @pl.when(i > 0)
        def _():
            start_copy(c, ctx).start()

    start_in[ctx] = start_out[ctx]
    inside(cut[2], cut[3])

    far = -steps * block.astype(jnp.float32)

    @functools.partial(each, nctx)
    def _(i):
        c = slot(i)

        @pl.when(i > 0)
        def _():
            start_copy(c, c).wait_recv()

        fetch(q_hbm, qbuf, q_sem, c).wait()

        @functools.partial(each, groups)
        def _(j):
            g = c * groups + j
            y = [inner[g, a] for a in range(steps)]
            for m in range(modes):
                p = wide(pows[g, pl.ds(m, 1), :])
                rate_m = wide(par[c, pl.ds(m, 1), lanes(j)])
                w = wide(par[c, pl.ds(modes + m, 1), lanes(j)])
                start = wide(start_in[c, pl.ds(m, 1), lanes(j)])
                lifted = (carry[g, m] + jnp.exp(far * rate_m) * start) * (w * p)
                for a in range(steps):
                    y[a] = y[a] + lifted
                    if a < steps - 1:
                        lifted = lifted * p
            for a in range(steps):
                turned[pl.ds(a, BLOCKS, stride=steps), :] = y[a]
            pre = turned[...].astype(jnp.bfloat16).astype(jnp.float32)
            gated = qbuf[c, :, lanes(j)].astype(jnp.float32) * pre
            obuf[c, :, lanes(j)] = gated.astype(jnp.bfloat16)

        store_out(c).start()

    @functools.partial(each, nctx)
    def _(i):
        store_out(slot(i)).wait()

    @functools.partial(each, nctx - 1)
    def _(i):
        c = slot(i + 1)
        par_copy(c, ctx).wait_send()
        state_copy(c, ctx).wait_send()
        start_copy(c, ctx).wait_send()

    @functools.partial(each, nseq - 1)
    def _(i):
        total_copy(lax.rem(seq + i + 1, nseq), seq).wait_send()


def local(nctx, nseq, queries, key_proj, value_proj, decay_rate, residue, skip_gain):
    modes, width = decay_rate.shape
    tokens, channels = queries.shape
    groups = channels // LANES
    weight = residue * jnp.sqrt(-jnp.expm1(-2.0 * decay_rate))
    rows = -(-(2 * modes + 1) // 8) * 8
    par = jnp.concatenate(
        [decay_rate, weight, jnp.broadcast_to(skip_gain[None], (rows - 2 * modes, width))], axis=0)
    f32, bf16 = jnp.float32, jnp.bfloat16
    any_spec = pl.BlockSpec(memory_space=pl.ANY)
    piece = pltpu.VMEM((nctx, tokens, width), bf16)
    state = pltpu.VMEM((nctx, modes, width), f32)
    sems = [pltpu.SemaphoreType.DMA((nctx,))] * 4 + [
        pltpu.SemaphoreType.DMA((n,)) for n in (nctx, nctx, nctx, nctx, nseq, nseq, nctx, nctx)]
    return pl.pallas_call(
        functools.partial(kernel, nctx, nseq, modes),
        out_shape=jax.ShapeDtypeStruct((tokens, channels), bf16),
        in_specs=[pl.BlockSpec(memory_space=pltpu.VMEM)] + [any_spec] * 3,
        out_specs=any_spec,
        scratch_shapes=[
            pltpu.VMEM((nctx, rows, width), f32),
            piece, piece, piece, piece,
            pltpu.VMEM((groups, tokens, LANES), f32),
            pltpu.VMEM((groups, tokens // BLOCKS, BLOCKS, LANES), f32),
            pltpu.VMEM((groups, modes, BLOCKS, LANES), f32),
            pltpu.VMEM((groups, 2 * modes, LANES), f32),
            state, state, state,
            pltpu.VMEM((nseq, modes, width), f32),
            state, state,
            pltpu.VMEM((tokens, LANES), f32),
        ] + sems,
        compiler_params=pltpu.CompilerParams(
            collective_id=0, has_side_effects=True, vmem_limit_bytes=48 * 1024 * 1024),
        cost_estimate=pl.CostEstimate(
            flops=tokens * channels * 90, bytes_accessed=8 * tokens * channels,
            transcendentals=groups * modes * LANES * 12),
    )(par, queries, key_proj, value_proj)


def solution(mesh):
    in_specs = (
        P(("seq", "ctx"), None),
        P(("seq", "ctx"), None),
        P(("seq", "ctx"), None),
        P(None, "ctx"),
        P(None, "ctx"),
        P("ctx"),
    )
    body = functools.partial(local, mesh.shape["ctx"], mesh.shape["seq"])
    return jax.shard_map(
        body, mesh=mesh, in_specs=in_specs, out_specs=P(("seq", "ctx"), None), check_vma=False)
```

```python
import functools

import jax
import jax.numpy as jnp
from jax import lax
from jax.experimental import pallas as pl
from jax.experimental.pallas import tpu as pltpu
from jax.sharding import PartitionSpec as P

LANES = 128
BLOCKS = 8
MESH = pl.DeviceIdType.MESH


def minus_expm1(x):
    series = jnp.ones_like(x)
    for n in range(9, 1, -1):
        series = 1.0 - series * x * (1.0 / n)
    return jnp.where(x < 0.25, x * series, 1.0 - jnp.exp(-x))


def kernel(
    nctx, nseq, modes, rate_in, residue_in, gain_in, q_hbm, k_hbm, v_hbm, out_hbm,
    rates, lifts, lift_out, kbuf, vbuf, qbuf, obuf, mixed, inner, carry, pows, state_out, state_in, local_start,
    totals, start_out, start_in, turned,
    k_sem, v_sem, q_sem, o_sem, rate_send, rate_recv, lift_send, lift_recv, st_send, st_recv, tot_send, tot_recv,
    go_send, go_recv,
):
    ctx, seq = lax.axis_index("ctx"), lax.axis_index("seq")
    tokens, width = kbuf.shape[1], kbuf.shape[2]
    groups = width // LANES
    steps = tokens // BLOCKS

    def slot(i):
        return lax.rem(ctx + i, nctx)

    def columns(c):
        return pl.ds(pl.multiple_of(c * width, LANES), width)

    def fetch(hbm, buf, sem, c):
        return pltpu.make_async_copy(hbm.at[:, columns(c)], buf.at[c], sem.at[c])

    def store_out(c):
        return pltpu.make_async_copy(obuf.at[c], out_hbm.at[:, columns(c)], o_sem.at[c])

    def swap(src, dst, to, send, recv, axis, other):
        return pltpu.make_async_remote_copy(
            src_ref=src, dst_ref=dst.at[to], send_sem=send.at[other], recv_sem=recv.at[to],
            device_id={axis: other}, device_id_type=MESH)

    def rate_copy(c, to):
        return swap(rate_in, rates, to, rate_send, rate_recv, "ctx", c)

    def lift_copy(c, to):
        return swap(lift_out, lifts, to, lift_send, lift_recv, "ctx", c)

    def state_copy(c, to):
        return swap(state_out.at[c], state_in, to, st_send, st_recv, "ctx", c)

    def total_copy(s, to):
        return swap(totals.at[seq], totals, to, tot_send, tot_recv, "seq", s)

    def start_copy(c, to):
        return swap(start_out.at[c], start_in, to, go_send, go_recv, "ctx", c)

    def each(count, body):
        lax.fori_loop(0, count, lambda i, x: (body(i), x)[1], 0)

    @functools.partial(each, nctx)
    def _(i):
        fetch(k_hbm, kbuf, k_sem, slot(i)).start()
        fetch(v_hbm, vbuf, v_sem, slot(i)).start()

    barrier = pltpu.get_barrier_semaphore()

    @functools.partial(each, nctx - 1)
    def _(i):
        pl.semaphore_signal(barrier, inc=1, device_id={"ctx": slot(i + 1)}, device_id_type=MESH)

    @functools.partial(each, nseq - 1)
    def _(i):
        pl.semaphore_signal(
            barrier, inc=1, device_id={"seq": lax.rem(seq + i + 1, nseq)}, device_id_type=MESH)

    pl.semaphore_wait(barrier, nctx + nseq - 2)

    @functools.partial(each, nctx - 1)
    def _(i):
        rate_copy(slot(i + 1), ctx).start()

    rate = rate_in[...]
    rates[ctx] = rate
    lift_out[0:modes, :] = residue_in[...] * jnp.sqrt(minus_expm1(2.0 * rate))
    lift_out[modes:, :] = jnp.broadcast_to(gain_in[...], (lift_out.shape[0] - modes, width))
    lifts[ctx] = lift_out[...]

    @functools.partial(each, nctx - 1)
    def _(i):
        lift_copy(slot(i + 1), ctx).start()

    @functools.partial(each, nctx)
    def _(i):
        fetch(q_hbm, qbuf, q_sem, slot(i)).start()

    block = lax.broadcasted_iota(jnp.int32, (BLOCKS, LANES), 0)

    def lanes(j):
        return pl.ds(pl.multiple_of(j * LANES, LANES), LANES)

    def wide(row):
        return jnp.broadcast_to(row, (BLOCKS, LANES))

    @functools.partial(each, nctx)
    def _(i):
        c = slot(i)

        @pl.when(i > 0)
        def _():
            rate_copy(c, c).wait_recv()

        fetch(k_hbm, kbuf, k_sem, c).wait()
        fetch(v_hbm, vbuf, v_sem, c).wait()

        @functools.partial(each, groups)
        def _(j):
            g = c * groups + j
            product = kbuf[c, :, lanes(j)].astype(jnp.float32) * vbuf[c, :, lanes(j)].astype(jnp.float32)
            mixed[g] = product.astype(jnp.bfloat16).astype(jnp.float32)
            rate = rates[c, :, lanes(j)]
            pows[g, 0:modes, :] = jnp.exp(-rate)
            pows[g, modes:2 * modes, :] = jnp.exp(-steps * rate)
            x = [mixed[g, pl.ds(a, BLOCKS, stride=steps), :] for a in range(steps)]
            for m in range(modes):
                p = wide(pows[g, pl.ds(m, 1), :])
                span = wide(pows[g, pl.ds(modes + m, 1), :])
                state = x[0]
                for a in range(1, steps):
                    state = state * p + x[a]
                shift = 1
                while shift < BLOCKS:
                    moved = pltpu.roll(state, shift, 0)
                    state = state + jnp.where(block >= shift, span, 0.0) * moved
                    span = span * span
                    shift *= 2
                carry[g, m] = jnp.where(block >= 1, pltpu.roll(state, 1, 0), 0.0)
                state_out[c, pl.ds(m, 1), lanes(j)] = state[BLOCKS - 1:, :]

        @pl.when(i > 0)
        def _():
            state_copy(c, ctx).start()

    def inside(first, last):
        def one(i):
            c = slot(i)

            @pl.when(i > 0)
            def _():
                lift_copy(c, c).wait_recv()

            @functools.partial(each, groups)
            def _(j):
                g = c * groups + j
                p = pows[g, 0:modes, :]
                w = lifts[c, 0:modes, lanes(j)]
                gain = lifts[c, pl.ds(modes, 1), lanes(j)]
                taps = []
                for a in range(steps):
                    tap = jnp.sum(w, axis=0, keepdims=True)
                    taps.append(wide(tap + gain if a == 0 else tap))
                    w = w * p
                x = [mixed[g, pl.ds(a, BLOCKS, stride=steps), :] for a in range(steps)]
                for a in range(steps):
                    y = taps[0] * x[a]
                    for b in range(a):
                        y = y + taps[a - b] * x[b]
                    inner[g, a] = y

        lax.fori_loop(first, last, lambda i, x: (one(i), x)[1], 0)

    cut = [0, (nctx * 3) // 8, (nctx * 6) // 8, nctx]
    inside(cut[0], cut[1])

    state_in[ctx] = state_out[ctx]

    @functools.partial(each, nctx - 1)
    def _(i):
        state_copy(slot(i + 1), slot(i + 1)).wait_recv()

    decay = jnp.exp(-tokens * rate)

    def link(s, state):
        local_start[s] = state
        return state * decay + state_in[s]

    totals[seq] = lax.fori_loop(0, nctx, link, jnp.zeros_like(rate))

    @functools.partial(each, nseq - 1)
    def _(i):
        total_copy(lax.rem(seq + i + 1, nseq), seq).start()

    inside(cut[1], cut[2])

    @functools.partial(each, nseq - 1)
    def _(i):
        s = lax.rem(seq + i + 1, nseq)
        total_copy(s, s).wait_recv()

    span_decay = jnp.exp(-(tokens * nctx) * rate)
    begin = lax.fori_loop(
        0, seq, lambda s, state: state * span_decay + totals[s], jnp.zeros_like(rate))

    @functools.partial(each, nctx)
    def _(i):
        c = slot(i)
        reach = jnp.exp(-(tokens * c).astype(jnp.float32) * rate)
        start_out[c] = local_start[c] + reach * begin

        @pl.when(i > 0)
        def _():
            start_copy(c, ctx).start()

    start_in[ctx] = start_out[ctx]
    inside(cut[2], cut[3])

    far = -steps * block.astype(jnp.float32)

    @functools.partial(each, nctx)
    def _(i):
        c = slot(i)

        @pl.when(i > 0)
        def _():
            start_copy(c, c).wait_recv()

        fetch(q_hbm, qbuf, q_sem, c).wait()

        @functools.partial(each, groups)
        def _(j):
            g = c * groups + j
            y = [inner[g, a] for a in range(steps)]
            for m in range(modes):
                p = wide(pows[g, pl.ds(m, 1), :])
                rate_m = wide(rates[c, pl.ds(m, 1), lanes(j)])
                w = wide(lifts[c, pl.ds(m, 1), lanes(j)])
                start = wide(start_in[c, pl.ds(m, 1), lanes(j)])
                lifted = (carry[g, m] + jnp.exp(far * rate_m) * start) * (w * p)
                for a in range(steps):
                    y[a] = y[a] + lifted
                    if a < steps - 1:
                        lifted = lifted * p
            for a in range(steps):
                turned[pl.ds(a, BLOCKS, stride=steps), :] = y[a]
            pre = turned[...].astype(jnp.bfloat16).astype(jnp.float32)
            gated = qbuf[c, :, lanes(j)].astype(jnp.float32) * pre
            obuf[c, :, lanes(j)] = gated.astype(jnp.bfloat16)

        store_out(c).start()

    @functools.partial(each, nctx)
    def _(i):
        store_out(slot(i)).wait()

    @functools.partial(each, nctx - 1)
    def _(i):
        c = slot(i + 1)
        rate_copy(c, ctx).wait_send()
        lift_copy(c, ctx).wait_send()
        state_copy(c, ctx).wait_send()
        start_copy(c, ctx).wait_send()

    @functools.partial(each, nseq - 1)
    def _(i):
        total_copy(lax.rem(seq + i + 1, nseq), seq).wait_send()


def local(nctx, nseq, queries, key_proj, value_proj, decay_rate, residue, skip_gain):
    modes, width = decay_rate.shape
    tokens, channels = queries.shape
    groups = channels // LANES
    rows = -(-(modes + 1) // 8) * 8
    f32, bf16 = jnp.float32, jnp.bfloat16
    any_spec = pl.BlockSpec(memory_space=pltpu.HBM)
    piece = pltpu.VMEM((nctx, tokens, width), bf16)
    state = pltpu.VMEM((nctx, modes, width), f32)
    sems = [pltpu.SemaphoreType.DMA((nctx,))] * 4 + [
        pltpu.SemaphoreType.DMA((n,)) for n in (nctx, nctx, nctx, nctx, nctx, nctx, nseq, nseq, nctx, nctx)]
    return pl.pallas_call(
        functools.partial(kernel, nctx, nseq, modes),
        out_shape=jax.ShapeDtypeStruct((tokens, channels), bf16),
        in_specs=[pl.BlockSpec(memory_space=pltpu.VMEM)] * 3 + [any_spec] * 3,
        out_specs=any_spec,
        scratch_shapes=[
            state,
            pltpu.VMEM((nctx, rows, width), f32),
            pltpu.VMEM((rows, width), f32),
            piece, piece, piece, piece,
            pltpu.VMEM((groups, tokens, LANES), f32),
            pltpu.VMEM((groups, tokens // BLOCKS, BLOCKS, LANES), f32),
            pltpu.VMEM((groups, modes, BLOCKS, LANES), f32),
            pltpu.VMEM((groups, 2 * modes, LANES), f32),
            state, state, state,
            pltpu.VMEM((nseq, modes, width), f32),
            state, state,
            pltpu.VMEM((tokens, LANES), f32),
        ] + sems,
        compiler_params=pltpu.CompilerParams(
            collective_id=0, has_side_effects=True, vmem_limit_bytes=60 * 1024 * 1024),
        cost_estimate=pl.CostEstimate(
            flops=tokens * channels * 90, bytes_accessed=8 * tokens * channels,
            transcendentals=groups * modes * LANES * 12),
    )(decay_rate, residue, skip_gain[None], queries, key_proj, value_proj)


def solution(mesh):
    in_specs = (
        P(("seq", "ctx"), None),
        P(("seq", "ctx"), None),
        P(("seq", "ctx"), None),
        P(None, "ctx"),
        P(None, "ctx"),
        P("ctx"),
    )
    body = functools.partial(local, mesh.shape["ctx"], mesh.shape["seq"])
    return jax.shard_map(
        body, mesh=mesh, in_specs=in_specs, out_specs=P(("seq", "ctx"), None), check_vma=False)
```

```python
import functools

import jax
import jax.numpy as jnp
from jax import lax
from jax.experimental import pallas as pl
from jax.experimental.pallas import tpu as pltpu
from jax.sharding import PartitionSpec as P

LANES = 128
BLOCKS = 8
MESH = pl.DeviceIdType.MESH


def minus_expm1(x):
    series = jnp.ones_like(x)
    for n in range(9, 1, -1):
        series = 1.0 - series * x * (1.0 / n)
    return jnp.where(x < 0.25, x * series, 1.0 - jnp.exp(-x))


def kernel(
    nctx, nseq, modes, halves, rate_in, residue_in, gain_in, q_hbm, k_hbm, v_hbm, out_hbm,
    rates, lifts, lift_out, kbuf, vbuf, qbuf, obuf, mixed, inner, carry, pows, state_out, state_in, local_start,
    totals, start_out, start_in, turned,
    k_sem, v_sem, q_sem, o_sem, rate_send, rate_recv, lift_send, lift_recv, st_send, st_recv, tot_send, tot_recv,
    go_send, go_recv,
):
    ctx, seq = lax.axis_index("ctx"), lax.axis_index("seq")
    tokens, width = kbuf.shape[1], kbuf.shape[2]
    groups = width // LANES
    steps = tokens // BLOCKS
    part = groups // halves
    half = part * LANES

    bits = [1 << n for n in range(nctx.bit_length() - 1)]
    signs = [b * (1 - 2 * lax.rem(ctx // b, 2)) for b in bits]

    def slot(i):
        place = ctx
        for b, sign in zip(bits, signs):
            place = place + lax.rem(i // b, 2) * sign
        return place

    def columns(c):
        return pl.ds(pl.multiple_of(c * width, LANES), width)

    def fetch(hbm, buf, sem, c):
        return pltpu.make_async_copy(hbm.at[:, columns(c)], buf.at[c], sem.at[c])

    def store_out(c):
        return pltpu.make_async_copy(obuf.at[c], out_hbm.at[:, columns(c)], o_sem.at[c])

    def swap(src, dst, to, send, recv, axis, other):
        return pltpu.make_async_remote_copy(
            src_ref=src, dst_ref=dst.at[to], send_sem=send.at[other], recv_sem=recv.at[to],
            device_id={axis: other}, device_id_type=MESH)

    def rate_copy(c, to):
        return swap(rate_in, rates, to, rate_send, rate_recv, "ctx", c)

    def lift_copy(c, to):
        return swap(lift_out, lifts, to, lift_send, lift_recv, "ctx", c)

    def state_copy(h, c, to):
        return swap(state_out.at[h, c], state_in.at[h], to, st_send.at[h], st_recv.at[h], "ctx", c)

    def total_copy(h, s, to):
        return swap(totals.at[h, seq], totals.at[h], to, tot_send.at[h], tot_recv.at[h], "seq", s)

    def start_copy(h, c, to):
        return swap(start_out.at[h, c], start_in.at[h], to, go_send.at[h], go_recv.at[h], "ctx", c)

    def each(count, body, first=0):
        lax.fori_loop(first, count, lambda i, x: (body(i), x)[1], 0)

    def plane(i):
        return lax.rem(seq + i + 1, nseq)

    barrier = pltpu.get_barrier_semaphore()

    @functools.partial(each, nctx - 1)
    def _(i):
        pl.semaphore_signal(barrier, inc=1, device_id={"ctx": slot(i + 1)}, device_id_type=MESH)

    @functools.partial(each, nseq - 1)
    def _(i):
        pl.semaphore_signal(barrier, inc=1, device_id={"seq": plane(i)}, device_id_type=MESH)

    @functools.partial(each, nctx)
    def _(i):
        fetch(k_hbm, kbuf, k_sem, slot(i)).start()
        fetch(v_hbm, vbuf, v_sem, slot(i)).start()

    rate = rate_in[...]
    rates[ctx] = rate
    lift_out[0:modes, :] = residue_in[...] * jnp.sqrt(minus_expm1(2.0 * rate))
    lift_out[modes:, :] = jnp.broadcast_to(gain_in[...], (lift_out.shape[0] - modes, width))
    lifts[ctx] = lift_out[...]

    pl.semaphore_wait(barrier, nctx + nseq - 2)

    @functools.partial(each, nctx - 1)
    def _(i):
        rate_copy(slot(i + 1), ctx).start()

    @functools.partial(each, nctx - 1)
    def _(i):
        lift_copy(slot(i + 1), ctx).start()

    @functools.partial(each, nctx)
    def _(i):
        fetch(q_hbm, qbuf, q_sem, slot(i)).start()

    block = lax.broadcasted_iota(jnp.int32, (BLOCKS, LANES), 0)

    def lanes(j):
        return pl.ds(pl.multiple_of(j * LANES, LANES), LANES)

    def wide(row):
        return jnp.broadcast_to(row, (BLOCKS, LANES))

    def ends(h, first, last):
        @functools.partial(each, last, first=first)
        def _(i):
            c = slot(i)

            if h == 0:
                @pl.when(i > 0)
                def _():
                    rate_copy(c, c).wait_recv()

                fetch(k_hbm, kbuf, k_sem, c).wait()
                fetch(v_hbm, vbuf, v_sem, c).wait()

            @functools.partial(each, part)
            def _(n):
                j = h * part + n
                g = c * groups + j
                product = kbuf[c, :, lanes(j)].astype(jnp.float32) * vbuf[c, :, lanes(j)].astype(jnp.float32)
                mixed[g] = product.astype(jnp.bfloat16).astype(jnp.float32)
                rate = rates[c, :, lanes(j)]
                pows[g, 0:modes, :] = jnp.exp(-rate)
                pows[g, modes:2 * modes, :] = jnp.exp(-steps * rate)
                x = [mixed[g, pl.ds(a, BLOCKS, stride=steps), :] for a in range(steps)]
                for m in range(modes):
                    p = wide(pows[g, pl.ds(m, 1), :])
                    span = wide(pows[g, pl.ds(modes + m, 1), :])
                    state = x[0]
                    for a in range(1, steps):
                        state = state * p + x[a]
                    shift = 1
                    while shift < BLOCKS:
                        moved = pltpu.roll(state, shift, 0)
                        state = state + jnp.where(block >= shift, span, 0.0) * moved
                        span = span * span
                        shift *= 2
                    carry[g, m] = jnp.where(block >= 1, pltpu.roll(state, 1, 0), 0.0)
                    state_out[h, c, pl.ds(m, 1), lanes(n)] = state[BLOCKS - 1:, :]

            @pl.when(i > 0)
            def _():
                state_copy(h, c, ctx).start()

    def inside(first, last):
        @functools.partial(each, last, first=first)
        def _(i):
            c = slot(i)

            @pl.when(i > 0)
            def _():
                lift_copy(c, c).wait_recv()

            @functools.partial(each, groups)
            def _(j):
                g = c * groups + j
                p = pows[g, 0:modes, :]
                w = lifts[c, 0:modes, lanes(j)]
                gain = lifts[c, pl.ds(modes, 1), lanes(j)]
                taps = []
                for a in range(steps):
                    tap = jnp.sum(w, axis=0, keepdims=True)
                    taps.append(wide(tap + gain if a == 0 else tap))
                    w = w * p
                x = [mixed[g, pl.ds(a, BLOCKS, stride=steps), :] for a in range(steps)]
                for a in range(steps):
                    y = taps[0] * x[a]
                    for b in range(a):
                        y = y + taps[a - b] * x[b]
                    inner[g, a] = y

    def gather_ends(h):
        state_in[h, ctx] = state_out[h, ctx]

        @functools.partial(each, nctx - 1)
        def _(i):
            state_copy(h, slot(i + 1), slot(i + 1)).wait_recv()

        decay = jnp.exp(-tokens * rate_in[:, h * half:(h + 1) * half])

        def link(s, state):
            local_start[h, s] = state
            return state * decay + state_in[h, s]

        totals[h, seq] = lax.fori_loop(0, nctx, link, jnp.zeros_like(decay))

        @functools.partial(each, nseq - 1)
        def _(i):
            total_copy(h, plane(i), seq).start()

    def send_starts(h):
        @functools.partial(each, nseq - 1)
        def _(i):
            total_copy(h, plane(i), plane(i)).wait_recv()

        rate = rate_in[:, h * half:(h + 1) * half]
        span_decay = jnp.exp(-(tokens * nctx) * rate)
        begin = lax.fori_loop(
            0, seq, lambda s, state: state * span_decay + totals[h, s], jnp.zeros_like(rate))

        @functools.partial(each, nctx)
        def _(i):
            c = slot(i)
            reach = jnp.exp(-(tokens * c).astype(jnp.float32) * rate)
            start_out[h, c] = local_start[h, c] + reach * begin

            @pl.when(i > 0)
            def _():
                start_copy(h, c, ctx).start()

        start_in[h, ctx] = start_out[h, ctx]

    far = -steps * block.astype(jnp.float32)

    def outputs(h):
        @functools.partial(each, nctx)
        def _(i):
            c = slot(i)

            @pl.when(i > 0)
            def _():
                start_copy(h, c, c).wait_recv()

            if h == 0:
                fetch(q_hbm, qbuf, q_sem, c).wait()

            @functools.partial(each, part)
            def _(n):
                j = h * part + n
                g = c * groups + j
                y = [inner[g, a] for a in range(steps)]
                for m in range(modes):
                    p = wide(pows[g, pl.ds(m, 1), :])
                    rate_m = wide(rates[c, pl.ds(m, 1), lanes(j)])
                    w = wide(lifts[c, pl.ds(m, 1), lanes(j)])
                    start = wide(start_in[h, c, pl.ds(m, 1), lanes(n)])
                    lifted = (carry[g, m] + jnp.exp(far * rate_m) * start) * (w * p)
                    for a in range(steps):
                        y[a] = y[a] + lifted
                        if a < steps - 1:
                            lifted = lifted * p
                for a in range(steps):
                    turned[pl.ds(a, BLOCKS, stride=steps), :] = y[a]
                pre = turned[...].astype(jnp.bfloat16).astype(jnp.float32)
                gated = qbuf[c, :, lanes(j)].astype(jnp.float32) * pre
                obuf[c, :, lanes(j)] = gated.astype(jnp.bfloat16)

            if h == halves - 1:
                store_out(c).start()

    ends(0, 0, nctx)
    if halves == 2:
        ends(1, 0, nctx // 2)
        gather_ends(0)
        ends(1, nctx // 2, nctx)
        inside(0, nctx // 2)
        gather_ends(1)
        send_starts(0)
        inside(nctx // 2, nctx)
        send_starts(1)
        outputs(0)
        outputs(1)
    else:
        inside(0, nctx // 4)
        gather_ends(0)
        inside(nctx // 4, nctx // 2)
        send_starts(0)
        inside(nctx // 2, nctx)
        outputs(0)

    @functools.partial(each, nctx)
    def _(i):
        store_out(slot(i)).wait()

    @functools.partial(each, nctx - 1)
    def _(i):
        c = slot(i + 1)
        rate_copy(c, ctx).wait_send()
        lift_copy(c, ctx).wait_send()
        for h in range(halves):
            state_copy(h, c, ctx).wait_send()
            start_copy(h, c, ctx).wait_send()

    @functools.partial(each, nseq - 1)
    def _(i):
        for h in range(halves):
            total_copy(h, plane(i), seq).wait_send()


def local(nctx, nseq, queries, key_proj, value_proj, decay_rate, residue, skip_gain):
    modes, width = decay_rate.shape
    tokens, channels = queries.shape
    groups = channels // LANES
    rows = -(-(modes + 1) // 8) * 8
    f32, bf16 = jnp.float32, jnp.bfloat16
    any_spec = pl.BlockSpec(memory_space=pltpu.HBM)
    piece = pltpu.VMEM((nctx, tokens, width), bf16)
    halves = 2 if (width // LANES) % 2 == 0 else 1
    state = pltpu.VMEM((halves, nctx, modes, width // halves), f32)
    sems = [pltpu.SemaphoreType.DMA((nctx,))] * 8 + [
        pltpu.SemaphoreType.DMA((halves, n)) for n in (nctx, nctx, nseq, nseq, nctx, nctx)]
    return pl.pallas_call(
        functools.partial(kernel, nctx, nseq, modes, halves),
        out_shape=jax.ShapeDtypeStruct((tokens, channels), bf16),
        in_specs=[pl.BlockSpec(memory_space=pltpu.VMEM)] * 3 + [any_spec] * 3,
        out_specs=any_spec,
        scratch_shapes=[
            pltpu.VMEM((nctx, modes, width), f32),
            pltpu.VMEM((nctx, rows, width), f32),
            pltpu.VMEM((rows, width), f32),
            piece, piece, piece, piece,
            pltpu.VMEM((groups, tokens, LANES), f32),
            pltpu.VMEM((groups, tokens // BLOCKS, BLOCKS, LANES), f32),
            pltpu.VMEM((groups, modes, BLOCKS, LANES), f32),
            pltpu.VMEM((groups, 2 * modes, LANES), f32),
            state, state, state,
            pltpu.VMEM((halves, nseq, modes, width // halves), f32),
            state, state,
            pltpu.VMEM((tokens, LANES), f32),
        ] + sems,
        compiler_params=pltpu.CompilerParams(
            collective_id=0, has_side_effects=True, vmem_limit_bytes=52 * 1024 * 1024),
        cost_estimate=pl.CostEstimate(
            flops=tokens * channels * 90, bytes_accessed=8 * tokens * channels,
            transcendentals=groups * modes * LANES * 12),
    )(decay_rate, residue, skip_gain[None], queries, key_proj, value_proj)


def solution(mesh):
    in_specs = (
        P(("seq", "ctx"), None),
        P(("seq", "ctx"), None),
        P(("seq", "ctx"), None),
        P(None, "ctx"),
        P(None, "ctx"),
        P("ctx"),
    )
    body = functools.partial(local, mesh.shape["ctx"], mesh.shape["seq"])
    return jax.shard_map(
        body, mesh=mesh, in_specs=in_specs, out_specs=P(("seq", "ctx"), None), check_vma=False)
```

```python
import functools

import jax
import jax.numpy as jnp
from jax import lax
from jax.experimental import pallas as pl
from jax.experimental.pallas import tpu as pltpu
from jax.sharding import PartitionSpec as P

LANES = 128
BLOCKS = 8
MESH = pl.DeviceIdType.MESH


def minus_expm1(x):
    series = jnp.ones_like(x)
    for n in range(9, 1, -1):
        series = 1.0 - series * x * (1.0 / n)
    return jnp.where(x < 0.25, x * series, 1.0 - jnp.exp(-x))


def kernel(
    nctx, nseq, modes, halves, rate_in, residue_in, gain_in, q_hbm, k_hbm, v_hbm, out_hbm,
    rates, lifts, lift_out, kbuf, vbuf, qbuf, obuf, mixed, inner, carry, pows, state_out, state_in, local_start,
    totals, start_out, start_in, turned, to_steps, to_tokens,
    k_sem, v_sem, q_sem, o_sem, rate_send, rate_recv, lift_send, lift_recv, st_send, st_recv, tot_send, tot_recv,
    go_send, go_recv,
):
    ctx, seq = lax.axis_index("ctx"), lax.axis_index("seq")
    tokens, width = kbuf.shape[1], kbuf.shape[2]
    groups = width // LANES
    steps = tokens // BLOCKS
    part = groups // halves
    half = part * LANES

    bits = [1 << n for n in range(nctx.bit_length() - 1)]
    signs = [b * (1 - 2 * lax.rem(ctx // b, 2)) for b in bits]

    def slot(i):
        place = ctx
        for b, sign in zip(bits, signs):
            place = place + lax.rem(i // b, 2) * sign
        return place

    def columns(c):
        return pl.ds(pl.multiple_of(c * width, LANES), width)

    def fetch(hbm, buf, sem, c):
        return pltpu.make_async_copy(hbm.at[:, columns(c)], buf.at[c], sem.at[c])

    def store_out(c):
        return pltpu.make_async_copy(obuf.at[c], out_hbm.at[:, columns(c)], o_sem.at[c])

    def swap(src, dst, to, send, recv, axis, other):
        return pltpu.make_async_remote_copy(
            src_ref=src, dst_ref=dst.at[to], send_sem=send.at[other], recv_sem=recv.at[to],
            device_id={axis: other}, device_id_type=MESH)

    def rate_copy(c, to):
        return swap(rate_in, rates, to, rate_send, rate_recv, "ctx", c)

    def lift_copy(c, to):
        return swap(lift_out, lifts, to, lift_send, lift_recv, "ctx", c)

    def state_copy(h, c, to):
        return swap(state_out.at[h, c], state_in.at[h], to, st_send.at[h], st_recv.at[h], "ctx", c)

    def total_copy(h, s, to):
        return swap(totals.at[h, seq], totals.at[h], to, tot_send.at[h], tot_recv.at[h], "seq", s)

    def start_copy(h, c, to):
        return swap(start_out.at[h, c], start_in.at[h], to, go_send.at[h], go_recv.at[h], "ctx", c)

    def each(count, body, first=0):
        lax.fori_loop(first, count, lambda i, x: (body(i), x)[1], 0)

    def plane(i):
        return lax.rem(seq + i + 1, nseq)

    barrier = pltpu.get_barrier_semaphore()

    @functools.partial(each, nctx - 1)
    def _(i):
        pl.semaphore_signal(barrier, inc=1, device_id={"ctx": slot(i + 1)}, device_id_type=MESH)

    @functools.partial(each, nseq - 1)
    def _(i):
        pl.semaphore_signal(barrier, inc=1, device_id={"seq": plane(i)}, device_id_type=MESH)

    @functools.partial(each, nctx)
    def _(i):
        fetch(k_hbm, kbuf, k_sem, slot(i)).start()
        fetch(v_hbm, vbuf, v_sem, slot(i)).start()

    rate = rate_in[...]
    rates[ctx] = rate
    lift_out[0:modes, :] = residue_in[...] * jnp.sqrt(minus_expm1(2.0 * rate))
    lift_out[modes:, :] = jnp.broadcast_to(gain_in[...], (lift_out.shape[0] - modes, width))
    lifts[ctx] = lift_out[...]

    row = lax.broadcasted_iota(jnp.int32, (tokens, tokens), 0)
    col = lax.broadcasted_iota(jnp.int32, (tokens, tokens), 1)
    to_steps[...] = jnp.where(
        col == (row % BLOCKS) * steps + row // BLOCKS, 1.0, 0.0).astype(jnp.bfloat16)
    to_tokens[...] = jnp.where(
        row == (col % BLOCKS) * steps + col // BLOCKS, 1.0, 0.0).astype(jnp.bfloat16)

    pl.semaphore_wait(barrier, nctx + nseq - 2)

    @functools.partial(each, nctx - 1)
    def _(i):
        rate_copy(slot(i + 1), ctx).start()

    @functools.partial(each, nctx - 1)
    def _(i):
        lift_copy(slot(i + 1), ctx).start()

    @functools.partial(each, nctx)
    def _(i):
        fetch(q_hbm, qbuf, q_sem, slot(i)).start()

    block = lax.broadcasted_iota(jnp.int32, (BLOCKS, LANES), 0)

    def lanes(j):
        return pl.ds(pl.multiple_of(j * LANES, LANES), LANES)

    def wide(row):
        return jnp.broadcast_to(row, (BLOCKS, LANES))

    def ends(h, first, last):
        @functools.partial(each, last, first=first)
        def _(i):
            c = slot(i)

            if h == 0:
                @pl.when(i > 0)
                def _():
                    rate_copy(c, c).wait_recv()

                fetch(k_hbm, kbuf, k_sem, c).wait()
                fetch(v_hbm, vbuf, v_sem, c).wait()

            own = pl.ds(h * half, half)
            product = kbuf[c, :, own] * vbuf[c, :, own]
            ordered = jnp.dot(to_steps[...], product, preferred_element_type=jnp.float32)
            for n in range(part):
                mixed[c * groups + h * part + n] = ordered[:, n * LANES:(n + 1) * LANES]

            @functools.partial(each, part)
            def _(n):
                j = h * part + n
                g = c * groups + j
                rate = rates[c, :, lanes(j)]
                pows[g, 0:modes, :] = jnp.exp(-rate)
                pows[g, modes:2 * modes, :] = jnp.exp(-steps * rate)
                x = [mixed[g, a * BLOCKS:(a + 1) * BLOCKS, :] for a in range(steps)]
                for m in range(modes):
                    p = wide(pows[g, pl.ds(m, 1), :])
                    span = wide(pows[g, pl.ds(modes + m, 1), :])
                    state = x[0]
                    for a in range(1, steps):
                        state = state * p + x[a]
                    shift = 1
                    while shift < BLOCKS:
                        moved = pltpu.roll(state, shift, 0)
                        state = state + jnp.where(block >= shift, span, 0.0) * moved
                        span = span * span
                        shift *= 2
                    carry[g, m] = jnp.where(block >= 1, pltpu.roll(state, 1, 0), 0.0)
                    state_out[h, c, pl.ds(m, 1), lanes(n)] = state[BLOCKS - 1:, :]

            @pl.when(i > 0)
            def _():
                state_copy(h, c, ctx).start()

    def inside(first, last):
        @functools.partial(each, last, first=first)
        def _(i):
            c = slot(i)

            @pl.when(i > 0)
            def _():
                lift_copy(c, c).wait_recv()

            @functools.partial(each, groups)
            def _(j):
                g = c * groups + j
                p = pows[g, 0:modes, :]
                w = lifts[c, 0:modes, lanes(j)]
                gain = lifts[c, pl.ds(modes, 1), lanes(j)]
                taps = []
                for a in range(steps):
                    tap = jnp.sum(w, axis=0, keepdims=True)
                    taps.append(wide(tap + gain if a == 0 else tap))
                    w = w * p
                x = [mixed[g, a * BLOCKS:(a + 1) * BLOCKS, :] for a in range(steps)]
                for a in range(steps):
                    y = taps[0] * x[a]
                    for b in range(a):
                        y = y + taps[a - b] * x[b]
                    inner[g, a] = y

    def gather_ends(h):
        state_in[h, ctx] = state_out[h, ctx]

        @functools.partial(each, nctx - 1)
        def _(i):
            state_copy(h, slot(i + 1), slot(i + 1)).wait_recv()

        decay = jnp.exp(-tokens * rate_in[:, h * half:(h + 1) * half])

        def link(s, state):
            local_start[h, s] = state
            return state * decay + state_in[h, s]

        totals[h, seq] = lax.fori_loop(0, nctx, link, jnp.zeros_like(decay))

        @functools.partial(each, nseq - 1)
        def _(i):
            total_copy(h, plane(i), seq).start()

    def send_starts(h):
        @functools.partial(each, nseq - 1)
        def _(i):
            total_copy(h, plane(i), plane(i)).wait_recv()

        rate = rate_in[:, h * half:(h + 1) * half]
        span_decay = jnp.exp(-(tokens * nctx) * rate)
        begin = lax.fori_loop(
            0, seq, lambda s, state: state * span_decay + totals[h, s], jnp.zeros_like(rate))

        @functools.partial(each, nctx)
        def _(i):
            c = slot(i)
            reach = jnp.exp(-(tokens * c).astype(jnp.float32) * rate)
            start_out[h, c] = local_start[h, c] + reach * begin

            @pl.when(i > 0)
            def _():
                start_copy(h, c, ctx).start()

        start_in[h, ctx] = start_out[h, ctx]

    far = -steps * block.astype(jnp.float32)

    def outputs(h):
        @functools.partial(each, nctx)
        def _(i):
            c = slot(i)

            @pl.when(i > 0)
            def _():
                start_copy(h, c, c).wait_recv()

            if h == 0:
                fetch(q_hbm, qbuf, q_sem, c).wait()

            @functools.partial(each, part)
            def _(n):
                j = h * part + n
                g = c * groups + j
                y = [inner[g, a] for a in range(steps)]
                for m in range(modes):
                    p = wide(pows[g, pl.ds(m, 1), :])
                    rate_m = wide(rates[c, pl.ds(m, 1), lanes(j)])
                    w = wide(lifts[c, pl.ds(m, 1), lanes(j)])
                    start = wide(start_in[h, c, pl.ds(m, 1), lanes(n)])
                    lifted = (carry[g, m] + jnp.exp(far * rate_m) * start) * (w * p)
                    for a in range(steps):
                        y[a] = y[a] + lifted
                        if a < steps - 1:
                            lifted = lifted * p
                turned[:, lanes(n)] = jnp.concatenate(y, axis=0).astype(jnp.bfloat16)

            pre = jnp.dot(to_tokens[...], turned[...], preferred_element_type=jnp.float32)
            own = pl.ds(h * half, half)
            obuf[c, :, own] = qbuf[c, :, own] * pre.astype(jnp.bfloat16)

            if h == halves - 1:
                store_out(c).start()

    ends(0, 0, nctx)
    if halves == 2:
        ends(1, 0, nctx // 2)
        gather_ends(0)
        ends(1, nctx // 2, nctx)
        inside(0, nctx // 2)
        gather_ends(1)
        send_starts(0)
        inside(nctx // 2, nctx)
        send_starts(1)
        outputs(0)
        outputs(1)
    else:
        inside(0, nctx // 4)
        gather_ends(0)
        inside(nctx // 4, nctx // 2)
        send_starts(0)
        inside(nctx // 2, nctx)
        outputs(0)

    @functools.partial(each, nctx)
    def _(i):
        store_out(slot(i)).wait()

    @functools.partial(each, nctx - 1)
    def _(i):
        c = slot(i + 1)
        rate_copy(c, ctx).wait_send()
        lift_copy(c, ctx).wait_send()
        for h in range(halves):
            state_copy(h, c, ctx).wait_send()
            start_copy(h, c, ctx).wait_send()

    @functools.partial(each, nseq - 1)
    def _(i):
        for h in range(halves):
            total_copy(h, plane(i), seq).wait_send()


def local(nctx, nseq, queries, key_proj, value_proj, decay_rate, residue, skip_gain):
    modes, width = decay_rate.shape
    tokens, channels = queries.shape
    groups = channels // LANES
    rows = -(-(modes + 1) // 8) * 8
    f32, bf16 = jnp.float32, jnp.bfloat16
    any_spec = pl.BlockSpec(memory_space=pltpu.HBM)
    piece = pltpu.VMEM((nctx, tokens, width), bf16)
    halves = 2 if (width // LANES) % 2 == 0 else 1
    state = pltpu.VMEM((halves, nctx, modes, width // halves), f32)
    sems = [pltpu.SemaphoreType.DMA((nctx,))] * 8 + [
        pltpu.SemaphoreType.DMA((halves, n)) for n in (nctx, nctx, nseq, nseq, nctx, nctx)]
    return pl.pallas_call(
        functools.partial(kernel, nctx, nseq, modes, halves),
        out_shape=jax.ShapeDtypeStruct((tokens, channels), bf16),
        in_specs=[pl.BlockSpec(memory_space=pltpu.VMEM)] * 3 + [any_spec] * 3,
        out_specs=any_spec,
        scratch_shapes=[
            pltpu.VMEM((nctx, modes, width), f32),
            pltpu.VMEM((nctx, rows, width), f32),
            pltpu.VMEM((rows, width), f32),
            piece, piece, piece, piece,
            pltpu.VMEM((groups, tokens, LANES), f32),
            pltpu.VMEM((groups, tokens // BLOCKS, BLOCKS, LANES), f32),
            pltpu.VMEM((groups, modes, BLOCKS, LANES), f32),
            pltpu.VMEM((groups, 2 * modes, LANES), f32),
            state, state, state,
            pltpu.VMEM((halves, nseq, modes, width // halves), f32),
            state, state,
            pltpu.VMEM((tokens, width // halves), bf16),
            pltpu.VMEM((tokens, tokens), bf16),
            pltpu.VMEM((tokens, tokens), bf16),
        ] + sems,
        compiler_params=pltpu.CompilerParams(
            collective_id=0, has_side_effects=True, vmem_limit_bytes=60 * 1024 * 1024),
        cost_estimate=pl.CostEstimate(
            flops=tokens * channels * 90, bytes_accessed=8 * tokens * channels,
            transcendentals=groups * modes * LANES * 12),
    )(decay_rate, residue, skip_gain[None], queries, key_proj, value_proj)


def solution(mesh):
    in_specs = (
        P(("seq", "ctx"), None),
        P(("seq", "ctx"), None),
        P(("seq", "ctx"), None),
        P(None, "ctx"),
        P(None, "ctx"),
        P("ctx"),
    )
    body = functools.partial(local, mesh.shape["ctx"], mesh.shape["seq"])
    return jax.shard_map(
        body, mesh=mesh, in_specs=in_specs, out_specs=P(("seq", "ctx"), None), check_vma=False)
```

```python
import functools

import jax
import jax.numpy as jnp
from jax import lax
from jax.experimental import pallas as pl
from jax.experimental.pallas import tpu as pltpu
from jax.sharding import PartitionSpec as P

LANES = 128
BLOCKS = 8
MESH = pl.DeviceIdType.MESH


def minus_expm1(x):
    series = jnp.ones_like(x)
    for n in range(9, 1, -1):
        series = 1.0 - series * x * (1.0 / n)
    return jnp.where(x < 0.25, x * series, 1.0 - jnp.exp(-x))


def kernel(
    nctx, nseq, modes, halves, rate_in, residue_in, gain_in, q_hbm, k_hbm, v_hbm, out_hbm,
    rates, lifts, lift_out, kbuf, vbuf, qbuf, obuf, mixed, inner, carry, pows, state_out, state_in, local_start,
    totals, start_out, start_in, turned,
    k_sem, v_sem, q_sem, o_sem, rate_send, rate_recv, lift_send, lift_recv, st_send, st_recv, tot_send, tot_recv,
    go_send, go_recv,
):
    ctx, seq = lax.axis_index("ctx"), lax.axis_index("seq")
    tokens, width = kbuf.shape[1], kbuf.shape[2]
    groups = width // LANES
    steps = tokens // BLOCKS
    part = groups // halves
    half = part * LANES

    bits = [1 << n for n in range(nctx.bit_length() - 1)]
    signs = [b * (1 - 2 * lax.rem(ctx // b, 2)) for b in bits]

    def slot(i):
        place = ctx
        for b, sign in zip(bits, signs):
            place = place + lax.rem(i // b, 2) * sign
        return place

    def columns(c):
        return pl.ds(pl.multiple_of(c * width, LANES), width)

    def fetch(hbm, buf, sem, c):
        return pltpu.make_async_copy(hbm.at[:, columns(c)], buf.at[c], sem.at[c])

    def store_out(c):
        return pltpu.make_async_copy(obuf.at[c], out_hbm.at[:, columns(c)], o_sem.at[c])

    def swap(src, dst, to, send, recv, axis, other):
        return pltpu.make_async_remote_copy(
            src_ref=src, dst_ref=dst.at[to], send_sem=send.at[other], recv_sem=recv.at[to],
            device_id={axis: other}, device_id_type=MESH)

    def rate_copy(c, to):
        return swap(rate_in, rates, to, rate_send, rate_recv, "ctx", c)

    def lift_copy(c, to):
        return swap(lift_out, lifts, to, lift_send, lift_recv, "ctx", c)

    def state_copy(h, c, to):
        return swap(state_out.at[h, c], state_in.at[h], to, st_send.at[h], st_recv.at[h], "ctx", c)

    def total_copy(h, s, to):
        return swap(totals.at[h, seq], totals.at[h], to, tot_send.at[h], tot_recv.at[h], "seq", s)

    def start_copy(h, c, to):
        return swap(start_out.at[h, c], start_in.at[h], to, go_send.at[h], go_recv.at[h], "ctx", c)

    def each(count, body, first=0):
        lax.fori_loop(first, count, lambda i, x: (body(i), x)[1], 0)

    def plane(i):
        return lax.rem(seq + i + 1, nseq)

    barrier = pltpu.get_barrier_semaphore()

    @functools.partial(each, nctx - 1)
    def _(i):
        pl.semaphore_signal(barrier, inc=1, device_id={"ctx": slot(i + 1)}, device_id_type=MESH)

    @functools.partial(each, nseq - 1)
    def _(i):
        pl.semaphore_signal(barrier, inc=1, device_id={"seq": plane(i)}, device_id_type=MESH)

    @functools.partial(each, nctx)
    def _(i):
        fetch(k_hbm, kbuf, k_sem, slot(i)).start()
        fetch(v_hbm, vbuf, v_sem, slot(i)).start()

    rate = rate_in[...]
    rates[ctx] = rate
    lift_out[0:modes, :] = residue_in[...] * jnp.sqrt(minus_expm1(2.0 * rate))
    lift_out[modes:, :] = jnp.broadcast_to(gain_in[...], (lift_out.shape[0] - modes, width))
    lifts[ctx] = lift_out[...]

    pl.semaphore_wait(barrier, nctx + nseq - 2)

    @functools.partial(each, nctx - 1)
    def _(i):
        rate_copy(slot(i + 1), ctx).start()

    @functools.partial(each, nctx - 1)
    def _(i):
        lift_copy(slot(i + 1), ctx).start()

    @functools.partial(each, nctx)
    def _(i):
        fetch(q_hbm, qbuf, q_sem, slot(i)).start()

    block = lax.broadcasted_iota(jnp.int32, (BLOCKS, LANES), 0)

    def lanes(j):
        return pl.ds(pl.multiple_of(j * LANES, LANES), LANES)

    def wide(row):
        return jnp.broadcast_to(row, (BLOCKS, LANES))

    def ends(h, first, last):
        @functools.partial(each, last, first=first)
        def _(i):
            c = slot(i)

            if h == 0:
                @pl.when(i > 0)
                def _():
                    rate_copy(c, c).wait_recv()

                fetch(k_hbm, kbuf, k_sem, c).wait()
                fetch(v_hbm, vbuf, v_sem, c).wait()

            @functools.partial(each, part)
            def _(n):
                j = h * part + n
                g = c * groups + j
                mixed[g] = (kbuf[c, :, lanes(j)] * vbuf[c, :, lanes(j)]).astype(jnp.float32)
                rate = rates[c, :, lanes(j)]
                pows[g, 0:modes, :] = jnp.exp(-rate)
                pows[g, modes:2 * modes, :] = jnp.exp(-steps * rate)
                p = [wide(pows[g, pl.ds(m, 1), :]) for m in range(modes)]
                state = [mixed[g, pl.ds(0, BLOCKS, stride=steps), :]] * modes
                for a in range(1, steps):
                    x = mixed[g, pl.ds(a, BLOCKS, stride=steps), :]
                    state = [state[m] * p[m] + x for m in range(modes)]
                span = [wide(pows[g, pl.ds(modes + m, 1), :]) for m in range(modes)]
                shift = 1
                while shift < BLOCKS:
                    moved = [pltpu.roll(one, shift, 0) for one in state]
                    state = [
                        state[m] + jnp.where(block >= shift, span[m], 0.0) * moved[m] for m in range(modes)]
                    shift *= 2
                    if shift < BLOCKS:
                        span = [one * one for one in span]
                moved = [pltpu.roll(one, 1, 0) for one in state]
                for m in range(modes):
                    carry[g, m] = jnp.where(block >= 1, moved[m], 0.0)
                    state_out[h, c, pl.ds(m, 1), lanes(n)] = state[m][BLOCKS - 1:, :]

            @pl.when(i > 0)
            def _():
                state_copy(h, c, ctx).start()

    def inside(first, last):
        @functools.partial(each, last, first=first)
        def _(i):
            c = slot(i)

            @pl.when(i > 0)
            def _():
                lift_copy(c, c).wait_recv()

            @functools.partial(each, groups)
            def _(j):
                g = c * groups + j
                p = pows[g, 0:modes, :]
                w = lifts[c, 0:modes, lanes(j)]
                gain = lifts[c, pl.ds(modes, 1), lanes(j)]
                taps = []
                for a in range(steps):
                    tap = jnp.sum(w, axis=0, keepdims=True)
                    taps.append(wide(tap + gain if a == 0 else tap))
                    w = w * p
                    lifted = w if a == 0 else lifted
                y = [taps[a] * mixed[g, pl.ds(0, BLOCKS, stride=steps), :] for a in range(steps)]
                for b in range(1, steps):
                    x = mixed[g, pl.ds(b, BLOCKS, stride=steps), :]
                    for a in range(b, steps):
                        y[a] = y[a] + taps[a - b] * x
                pows[g, modes:2 * modes, :] = lifted
                for a in range(steps):
                    inner[g, a] = y[a]

    def gather_ends(h):
        state_in[h, ctx] = state_out[h, ctx]

        @functools.partial(each, nctx - 1)
        def _(i):
            state_copy(h, slot(i + 1), slot(i + 1)).wait_recv()

        decay = jnp.exp(-tokens * rate_in[:, h * half:(h + 1) * half])

        def link(s, state):
            local_start[h, s] = state
            return state * decay + state_in[h, s]

        totals[h, seq] = lax.fori_loop(0, nctx, link, jnp.zeros_like(decay))

        @functools.partial(each, nseq - 1)
        def _(i):
            total_copy(h, plane(i), seq).start()

    def send_starts(h):
        @functools.partial(each, nseq - 1)
        def _(i):
            total_copy(h, plane(i), plane(i)).wait_recv()

        rate = rate_in[:, h * half:(h + 1) * half]
        span_decay = jnp.exp(-(tokens * nctx) * rate)
        begin = lax.fori_loop(
            0, seq, lambda s, state: state * span_decay + totals[h, s], jnp.zeros_like(rate))

        @functools.partial(each, nctx)
        def _(i):
            c = slot(i)
            reach = jnp.exp(-(tokens * c).astype(jnp.float32) * rate)
            start_out[h, c] = local_start[h, c] + reach * begin

            @pl.when(i > 0)
            def _():
                start_copy(h, c, ctx).start()

        start_in[h, ctx] = start_out[h, ctx]

    far = -steps * block.astype(jnp.float32)

    def outputs(h):
        @functools.partial(each, nctx)
        def _(i):
            c = slot(i)

            @pl.when(i > 0)
            def _():
                start_copy(h, c, c).wait_recv()

            if h == 0:
                fetch(q_hbm, qbuf, q_sem, c).wait()

            @functools.partial(each, part)
            def _(n):
                j = h * part + n
                g = c * groups + j
                begin = [
                    jnp.exp(far * wide(rates[c, pl.ds(m, 1), lanes(j)]))
                    * wide(start_in[h, c, pl.ds(m, 1), lanes(n)])
                    for m in range(modes)]
                lifted = [
                    (carry[g, m] + begin[m]) * wide(pows[g, pl.ds(modes + m, 1), :]) for m in range(modes)]
                p = [wide(pows[g, pl.ds(m, 1), :]) for m in range(modes)]
                y = []
                for a in range(steps):
                    terms = [inner[g, a]] + lifted
                    while len(terms) > 1:
                        terms = [sum(terms[n:n + 2][1:], terms[n]) for n in range(0, len(terms), 2)]
                    y += terms
                    if a < steps - 1:
                        lifted = [lifted[m] * p[m] for m in range(modes)]
                for a in range(steps):
                    turned[pl.ds(a, BLOCKS, stride=steps), :] = y[a]
                obuf[c, :, lanes(j)] = qbuf[c, :, lanes(j)] * turned[...].astype(jnp.bfloat16)

            if h == halves - 1:
                store_out(c).start()

    ends(0, 0, nctx)
    if halves == 2:
        ends(1, 0, nctx // 2)
        gather_ends(0)
        ends(1, nctx // 2, nctx)
        inside(0, nctx // 2)
        gather_ends(1)
        send_starts(0)
        inside(nctx // 2, nctx)
        send_starts(1)
        outputs(0)
        outputs(1)
    else:
        inside(0, nctx // 4)
        gather_ends(0)
        inside(nctx // 4, nctx // 2)
        send_starts(0)
        inside(nctx // 2, nctx)
        outputs(0)

    @functools.partial(each, nctx)
    def _(i):
        store_out(slot(i)).wait()

    @functools.partial(each, nctx - 1)
    def _(i):
        c = slot(i + 1)
        rate_copy(c, ctx).wait_send()
        lift_copy(c, ctx).wait_send()
        for h in range(halves):
            state_copy(h, c, ctx).wait_send()
            start_copy(h, c, ctx).wait_send()

    @functools.partial(each, nseq - 1)
    def _(i):
        for h in range(halves):
            total_copy(h, plane(i), seq).wait_send()


def local(nctx, nseq, queries, key_proj, value_proj, decay_rate, residue, skip_gain):
    modes, width = decay_rate.shape
    tokens, channels = queries.shape
    groups = channels // LANES
    rows = -(-(modes + 1) // 8) * 8
    f32, bf16 = jnp.float32, jnp.bfloat16
    any_spec = pl.BlockSpec(memory_space=pltpu.HBM)
    piece = pltpu.VMEM((nctx, tokens, width), bf16)
    halves = 2 if (width // LANES) % 2 == 0 else 1
    state = pltpu.VMEM((halves, nctx, modes, width // halves), f32)
    sems = [pltpu.SemaphoreType.DMA((nctx,))] * 8 + [
        pltpu.SemaphoreType.DMA((halves, n)) for n in (nctx, nctx, nseq, nseq, nctx, nctx)]
    return pl.pallas_call(
        functools.partial(kernel, nctx, nseq, modes, halves),
        out_shape=jax.ShapeDtypeStruct((tokens, channels), bf16),
        in_specs=[pl.BlockSpec(memory_space=pltpu.VMEM)] * 3 + [any_spec] * 3,
        out_specs=any_spec,
        scratch_shapes=[
            pltpu.VMEM((nctx, modes, width), f32),
            pltpu.VMEM((nctx, rows, width), f32),
            pltpu.VMEM((rows, width), f32),
            piece, piece, piece, piece,
            pltpu.VMEM((groups, tokens, LANES), f32),
            pltpu.VMEM((groups, tokens // BLOCKS, BLOCKS, LANES), f32),
            pltpu.VMEM((groups, modes, BLOCKS, LANES), f32),
            pltpu.VMEM((groups, 2 * modes, LANES), f32),
            state, state, state,
            pltpu.VMEM((halves, nseq, modes, width // halves), f32),
            state, state,
            pltpu.VMEM((tokens, LANES), f32),
        ] + sems,
        compiler_params=pltpu.CompilerParams(
            collective_id=0, has_side_effects=True, vmem_limit_bytes=60 * 1024 * 1024),
        cost_estimate=pl.CostEstimate(
            flops=tokens * channels * 90, bytes_accessed=8 * tokens * channels,
            transcendentals=groups * modes * LANES * 12),
    )(decay_rate, residue, skip_gain[None], queries, key_proj, value_proj)


def solution(mesh):
    in_specs = (
        P(("seq", "ctx"), None),
        P(("seq", "ctx"), None),
        P(("seq", "ctx"), None),
        P(None, "ctx"),
        P(None, "ctx"),
        P("ctx"),
    )
    body = functools.partial(local, mesh.shape["ctx"], mesh.shape["seq"])
    return jax.shard_map(
        body, mesh=mesh, in_specs=in_specs, out_specs=P(("seq", "ctx"), None), check_vma=False)
```

```python
import functools

import jax
import jax.numpy as jnp
from jax import lax
from jax.experimental import pallas as pl
from jax.experimental.pallas import tpu as pltpu
from jax.sharding import PartitionSpec as P

LANES = 128
BLOCKS = 8
MESH = pl.DeviceIdType.MESH


def minus_expm1(x):
    series = jnp.ones_like(x)
    for n in range(9, 1, -1):
        series = 1.0 - series * x * (1.0 / n)
    return jnp.where(x < 0.25, x * series, 1.0 - jnp.exp(-x))


def kernel(
    nctx, nseq, modes, halves, rate_in, residue_in, gain_in, q_hbm, k_hbm, v_hbm, out_hbm,
    rates, lifts, lift_out, kbuf, vbuf, qbuf, obuf, mixed, inner, carry, pows, state_out, state_in, local_start,
    totals, start_out, start_in, turned,
    k_sem, v_sem, q_sem, o_sem, rate_send, rate_recv, lift_send, lift_recv, st_send, st_recv, tot_send, tot_recv,
    go_send, go_recv, rate_fwd, lift_fwd,
):
    ctx, seq = lax.axis_index("ctx"), lax.axis_index("seq")
    tokens, width = kbuf.shape[1], kbuf.shape[2]
    groups = width // LANES
    steps = tokens // BLOCKS
    part = groups // halves
    half = part * LANES

    bits = [1 << n for n in range(nctx.bit_length() - 1)]
    signs = [b * (1 - 2 * lax.rem(ctx // b, 2)) for b in bits]

    def slot(i):
        place = ctx
        for b, sign in zip(bits, signs):
            place = place + lax.rem(i // b, 2) * sign
        return place

    def columns(c):
        return pl.ds(pl.multiple_of(c * width, LANES), width)

    def fetch(hbm, buf, sem, c):
        return pltpu.make_async_copy(hbm.at[:, columns(c)], buf.at[c], sem.at[c])

    def store_out(c):
        return pltpu.make_async_copy(obuf.at[c], out_hbm.at[:, columns(c)], o_sem.at[c])

    def swap(src, dst, to, send, recv, axis, other):
        return pltpu.make_async_remote_copy(
            src_ref=src, dst_ref=dst.at[to], send_sem=send.at[other], recv_sem=recv.at[to],
            device_id={axis: other}, device_id_type=MESH)

    def rate_copy(c, to):
        return swap(rate_in, rates, to, rate_send, rate_recv, "ctx", c)

    def lift_copy(c, to):
        return swap(lift_out, lifts, to, lift_send, lift_recv, "ctx", c)

    def hand_on(buf, c, send, recv):
        return pltpu.make_async_remote_copy(
            src_ref=buf.at[c], dst_ref=buf.at[c], send_sem=send.at[c], recv_sem=recv.at[c],
            device_id={"ctx": slot(1)}, device_id_type=MESH)

    def rate_on(c):
        return hand_on(rates, c, rate_fwd, rate_recv)

    def lift_on(c):
        return hand_on(lifts, c, lift_fwd, lift_recv)

    def near(i):
        return slot(jnp.where(i == 0, 1, 2 * i))

    def state_copy(h, c, to):
        return swap(state_out.at[h, c], state_in.at[h], to, st_send.at[h], st_recv.at[h], "ctx", c)

    def total_copy(h, s, to):
        return swap(totals.at[h, seq], totals.at[h], to, tot_send.at[h], tot_recv.at[h], "seq", s)

    def start_copy(h, c, to):
        return swap(start_out.at[h, c], start_in.at[h], to, go_send.at[h], go_recv.at[h], "ctx", c)

    def each(count, body, first=0):
        lax.fori_loop(first, count, lambda i, x: (body(i), x)[1], 0)

    def plane(i):
        return lax.rem(seq + i + 1, nseq)

    barrier = pltpu.get_barrier_semaphore()

    @functools.partial(each, nctx - 1)
    def _(i):
        pl.semaphore_signal(barrier, inc=1, device_id={"ctx": slot(i + 1)}, device_id_type=MESH)

    @functools.partial(each, nseq - 1)
    def _(i):
        pl.semaphore_signal(barrier, inc=1, device_id={"seq": plane(i)}, device_id_type=MESH)

    @functools.partial(each, nctx)
    def _(i):
        fetch(k_hbm, kbuf, k_sem, slot(i)).start()
        fetch(v_hbm, vbuf, v_sem, slot(i)).start()

    rate = rate_in[...]
    rates[ctx] = rate
    lift_out[0:modes, :] = residue_in[...] * jnp.sqrt(minus_expm1(2.0 * rate))
    lift_out[modes:, :] = jnp.broadcast_to(gain_in[...], (lift_out.shape[0] - modes, width))
    lifts[ctx] = lift_out[...]

    pl.semaphore_wait(barrier, nctx + nseq - 2)

    @functools.partial(each, nctx // 2)
    def _(i):
        rate_copy(near(i), ctx).start()

    @functools.partial(each, nctx // 2)
    def _(i):
        lift_copy(near(i), ctx).start()

    @functools.partial(each, nctx)
    def _(i):
        fetch(q_hbm, qbuf, q_sem, slot(i)).start()

    block = lax.broadcasted_iota(jnp.int32, (BLOCKS, LANES), 0)

    def lanes(j):
        return pl.ds(pl.multiple_of(j * LANES, LANES), LANES)

    def wide(row):
        return jnp.broadcast_to(row, (BLOCKS, LANES))

    def ends(h, first, last):
        @functools.partial(each, last, first=first)
        def _(i):
            c = slot(i)

            if h == 0:
                @pl.when(i > 0)
                def _():
                    rate_copy(c, c).wait_recv()

                    @pl.when(lax.rem(i, 2) == 0)
                    def _():
                        rate_on(c).start()

                fetch(k_hbm, kbuf, k_sem, c).wait()
                fetch(v_hbm, vbuf, v_sem, c).wait()

            @functools.partial(each, part)
            def _(n):
                j = h * part + n
                g = c * groups + j
                mixed[g] = (kbuf[c, :, lanes(j)] * vbuf[c, :, lanes(j)]).astype(jnp.float32)
                rate = rates[c, :, lanes(j)]
                pows[g, 0:modes, :] = jnp.exp(-rate)
                pows[g, modes:2 * modes, :] = jnp.exp(-steps * rate)
                p = [wide(pows[g, pl.ds(m, 1), :]) for m in range(modes)]
                state = [mixed[g, pl.ds(0, BLOCKS, stride=steps), :]] * modes
                for a in range(1, steps):
                    x = mixed[g, pl.ds(a, BLOCKS, stride=steps), :]
                    state = [state[m] * p[m] + x for m in range(modes)]
                span = [wide(pows[g, pl.ds(modes + m, 1), :]) for m in range(modes)]
                shift = 1
                while shift < BLOCKS:
                    moved = [pltpu.roll(one, shift, 0) for one in state]
                    state = [
                        state[m] + jnp.where(block >= shift, span[m], 0.0) * moved[m] for m in range(modes)]
                    shift *= 2
                    if shift < BLOCKS:
                        span = [one * one for one in span]
                moved = [pltpu.roll(one, 1, 0) for one in state]
                for m in range(modes):
                    carry[g, m] = jnp.where(block >= 1, moved[m], 0.0)
                    state_out[h, c, pl.ds(m, 1), lanes(n)] = state[m][BLOCKS - 1:, :]

            @pl.when(i > 0)
            def _():
                state_copy(h, c, ctx).start()

    def inside(first, last):
        @functools.partial(each, last, first=first)
        def _(i):
            c = slot(i)

            @pl.when(i > 0)
            def _():
                lift_copy(c, c).wait_recv()

                @pl.when(lax.rem(i, 2) == 0)
                def _():
                    lift_on(c).start()

            @functools.partial(each, groups)
            def _(j):
                g = c * groups + j
                p = pows[g, 0:modes, :]
                w = lifts[c, 0:modes, lanes(j)]
                gain = lifts[c, pl.ds(modes, 1), lanes(j)]
                taps = []
                for a in range(steps):
                    tap = jnp.sum(w, axis=0, keepdims=True)
                    taps.append(wide(tap + gain if a == 0 else tap))
                    w = w * p
                    lifted = w if a == 0 else lifted
                y = [taps[a] * mixed[g, pl.ds(0, BLOCKS, stride=steps), :] for a in range(steps)]
                for b in range(1, steps):
                    x = mixed[g, pl.ds(b, BLOCKS, stride=steps), :]
                    for a in range(b, steps):
                        y[a] = y[a] + taps[a - b] * x
                pows[g, modes:2 * modes, :] = lifted
                for a in range(steps):
                    inner[g, a] = y[a]

    def gather_ends(h):
        state_in[h, ctx] = state_out[h, ctx]

        @functools.partial(each, nctx - 1)
        def _(i):
            state_copy(h, slot(i + 1), slot(i + 1)).wait_recv()

        decay = jnp.exp(-tokens * rate_in[:, h * half:(h + 1) * half])

        def link(s, state):
            local_start[h, s] = state
            return state * decay + state_in[h, s]

        totals[h, seq] = lax.fori_loop(0, nctx, link, jnp.zeros_like(decay))

        @functools.partial(each, nseq - 1)
        def _(i):
            total_copy(h, plane(i), seq).start()

    def send_starts(h):
        @functools.partial(each, nseq - 1)
        def _(i):
            total_copy(h, plane(i), plane(i)).wait_recv()

        rate = rate_in[:, h * half:(h + 1) * half]
        span_decay = jnp.exp(-(tokens * nctx) * rate)
        begin = lax.fori_loop(
            0, seq, lambda s, state: state * span_decay + totals[h, s], jnp.zeros_like(rate))

        @functools.partial(each, nctx)
        def _(i):
            c = slot(i)
            reach = jnp.exp(-(tokens * c).astype(jnp.float32) * rate)
            start_out[h, c] = local_start[h, c] + reach * begin

            @pl.when(i > 0)
            def _():
                start_copy(h, c, ctx).start()

        start_in[h, ctx] = start_out[h, ctx]

    far = -steps * block.astype(jnp.float32)

    def outputs(h):
        @functools.partial(each, nctx)
        def _(i):
            c = slot(i)

            @pl.when(i > 0)
            def _():
                start_copy(h, c, c).wait_recv()

            if h == 0:
                fetch(q_hbm, qbuf, q_sem, c).wait()

            @functools.partial(each, part)
            def _(n):
                j = h * part + n
                g = c * groups + j
                begin = [
                    jnp.exp(far * wide(rates[c, pl.ds(m, 1), lanes(j)]))
                    * wide(start_in[h, c, pl.ds(m, 1), lanes(n)])
                    for m in range(modes)]
                lifted = [
                    (carry[g, m] + begin[m]) * wide(pows[g, pl.ds(modes + m, 1), :]) for m in range(modes)]
                p = [wide(pows[g, pl.ds(m, 1), :]) for m in range(modes)]
                y = []
                for a in range(steps):
                    terms = [inner[g, a]] + lifted
                    while len(terms) > 1:
                        terms = [sum(terms[n:n + 2][1:], terms[n]) for n in range(0, len(terms), 2)]
                    y += terms
                    if a < steps - 1:
                        lifted = [lifted[m] * p[m] for m in range(modes)]
                for a in range(steps):
                    turned[pl.ds(a, BLOCKS, stride=steps), :] = y[a]
                obuf[c, :, lanes(j)] = qbuf[c, :, lanes(j)] * turned[...].astype(jnp.bfloat16)

            if h == halves - 1:
                store_out(c).start()

    ends(0, 0, nctx)
    if halves == 2:
        ends(1, 0, nctx // 2)
        gather_ends(0)
        ends(1, nctx // 2, nctx)
        inside(0, nctx // 2)
        gather_ends(1)
        send_starts(0)
        inside(nctx // 2, nctx)
        send_starts(1)
        outputs(0)
        outputs(1)
    else:
        inside(0, nctx // 4)
        gather_ends(0)
        inside(nctx // 4, nctx // 2)
        send_starts(0)
        inside(nctx // 2, nctx)
        outputs(0)

    @functools.partial(each, nctx)
    def _(i):
        store_out(slot(i)).wait()

    @functools.partial(each, nctx - 1)
    def _(i):
        c = slot(i + 1)
        for h in range(halves):
            state_copy(h, c, ctx).wait_send()
            start_copy(h, c, ctx).wait_send()

    @functools.partial(each, nctx // 2)
    def _(i):
        rate_copy(near(i), ctx).wait_send()
        lift_copy(near(i), ctx).wait_send()

    @functools.partial(each, nctx // 2, first=1)
    def _(i):
        rate_on(near(i)).wait_send()
        lift_on(near(i)).wait_send()

    @functools.partial(each, nseq - 1)
    def _(i):
        for h in range(halves):
            total_copy(h, plane(i), seq).wait_send()


def local(nctx, nseq, queries, key_proj, value_proj, decay_rate, residue, skip_gain):
    modes, width = decay_rate.shape
    tokens, channels = queries.shape
    groups = channels // LANES
    rows = -(-(modes + 1) // 8) * 8
    f32, bf16 = jnp.float32, jnp.bfloat16
    any_spec = pl.BlockSpec(memory_space=pltpu.HBM)
    piece = pltpu.VMEM((nctx, tokens, width), bf16)
    halves = 2 if (width // LANES) % 2 == 0 else 1
    state = pltpu.VMEM((halves, nctx, modes, width // halves), f32)
    sems = [pltpu.SemaphoreType.DMA((nctx,))] * 8 + [
        pltpu.SemaphoreType.DMA((halves, n)) for n in (nctx, nctx, nseq, nseq, nctx, nctx)] + [
        pltpu.SemaphoreType.DMA((nctx,))] * 2
    return pl.pallas_call(
        functools.partial(kernel, nctx, nseq, modes, halves),
        out_shape=jax.ShapeDtypeStruct((tokens, channels), bf16),
        in_specs=[pl.BlockSpec(memory_space=pltpu.VMEM)] * 3 + [any_spec] * 3,
        out_specs=any_spec,
        scratch_shapes=[
            pltpu.VMEM((nctx, modes, width), f32),
            pltpu.VMEM((nctx, rows, width), f32),
            pltpu.VMEM((rows, width), f32),
            piece, piece, piece, piece,
            pltpu.VMEM((groups, tokens, LANES), f32),
            pltpu.VMEM((groups, tokens // BLOCKS, BLOCKS, LANES), f32),
            pltpu.VMEM((groups, modes, BLOCKS, LANES), f32),
            pltpu.VMEM((groups, 2 * modes, LANES), f32),
            state, state, state,
            pltpu.VMEM((halves, nseq, modes, width // halves), f32),
            state, state,
            pltpu.VMEM((tokens, LANES), f32),
        ] + sems,
        compiler_params=pltpu.CompilerParams(
            collective_id=0, has_side_effects=True, vmem_limit_bytes=60 * 1024 * 1024),
        cost_estimate=pl.CostEstimate(
            flops=tokens * channels * 90, bytes_accessed=8 * tokens * channels,
            transcendentals=groups * modes * LANES * 12),
    )(decay_rate, residue, skip_gain[None], queries, key_proj, value_proj)


def solution(mesh):
    in_specs = (
        P(("seq", "ctx"), None),
        P(("seq", "ctx"), None),
        P(("seq", "ctx"), None),
        P(None, "ctx"),
        P(None, "ctx"),
        P("ctx"),
    )
    body = functools.partial(local, mesh.shape["ctx"], mesh.shape["seq"])
    return jax.shard_map(
        body, mesh=mesh, in_specs=in_specs, out_specs=P(("seq", "ctx"), None), check_vma=False)
```

```python
import functools

import jax
import jax.numpy as jnp
from jax import lax
from jax.experimental import pallas as pl
from jax.experimental.pallas import tpu as pltpu
from jax.sharding import PartitionSpec as P

LANES = 128
BLOCKS = 8
MESH = pl.DeviceIdType.MESH


def minus_expm1(x):
    series = jnp.ones_like(x)
    for n in range(9, 1, -1):
        series = 1.0 - series * x * (1.0 / n)
    return jnp.where(x < 0.25, x * series, 1.0 - jnp.exp(-x))


def kernel(
    nctx, nseq, modes, halves, rate_in, residue_in, gain_in, q_hbm, k_hbm, v_hbm, out_hbm,
    rates, lifts, lift_out, kbuf, vbuf, qbuf, obuf, mixed, inner, carry, pows, state_out, state_in, local_start,
    totals, start_out, start_in, turned,
    k_sem, v_sem, q_sem, o_sem, rate_send, rate_recv, lift_send, lift_recv, st_send, st_recv, tot_send, tot_recv,
    go_send, go_recv, rate_fwd, lift_fwd,
):
    ctx, seq = lax.axis_index("ctx"), lax.axis_index("seq")
    tokens, width = kbuf.shape[1], kbuf.shape[2]
    groups = width // LANES
    steps = tokens // BLOCKS
    part = groups // halves
    half = part * LANES

    bits = [1 << n for n in range(nctx.bit_length() - 1)]
    signs = [b * (1 - 2 * lax.rem(ctx // b, 2)) for b in bits]

    def slot(i):
        place = ctx
        for b, sign in zip(bits, signs):
            place = place + lax.rem(i // b, 2) * sign
        return place

    def columns(c):
        return pl.ds(pl.multiple_of(c * width, LANES), width)

    def fetch(hbm, buf, sem, c):
        return pltpu.make_async_copy(hbm.at[:, columns(c)], buf.at[c], sem.at[c])

    def store_out(c):
        return pltpu.make_async_copy(obuf.at[c], out_hbm.at[:, columns(c)], o_sem.at[c])

    def swap(src, dst, to, send, recv, axis, other):
        return pltpu.make_async_remote_copy(
            src_ref=src, dst_ref=dst.at[to], send_sem=send.at[other], recv_sem=recv.at[to],
            device_id={axis: other}, device_id_type=MESH)

    def rate_copy(c, to):
        return swap(rate_in, rates, to, rate_send, rate_recv, "ctx", c)

    def lift_copy(c, to):
        return swap(lift_out, lifts, to, lift_send, lift_recv, "ctx", c)

    def hand_on(buf, c, send, recv):
        return pltpu.make_async_remote_copy(
            src_ref=buf.at[c], dst_ref=buf.at[c], send_sem=send.at[c], recv_sem=recv.at[c],
            device_id={"ctx": slot(1)}, device_id_type=MESH)

    def rate_on(c):
        return hand_on(rates, c, rate_fwd, rate_recv)

    def lift_on(c):
        return hand_on(lifts, c, lift_fwd, lift_recv)

    def near(i):
        return slot(jnp.where(i == 0, 1, 2 * i))

    def state_copy(h, c, to):
        return swap(state_out.at[h, c], state_in.at[h], to, st_send.at[h], st_recv.at[h], "ctx", c)

    def total_copy(h, s, to):
        return swap(totals.at[h, seq], totals.at[h], to, tot_send.at[h], tot_recv.at[h], "seq", s)

    def start_copy(h, c, to):
        return swap(start_out.at[h, c], start_in.at[h], to, go_send.at[h], go_recv.at[h], "ctx", c)

    def each(count, body, first=0):
        lax.fori_loop(first, count, lambda i, x: (body(i), x)[1], 0)

    def pairs(count, body):
        if count % 2:
            each(count, body)
        elif count == 2:
            for n in range(2):
                body(n)
        else:
            each(count // 2, lambda i: (body(2 * i), body(2 * i + 1)))

    def plane(i):
        return lax.rem(seq + i + 1, nseq)

    barrier = pltpu.get_barrier_semaphore()

    @functools.partial(each, nctx - 1)
    def _(i):
        pl.semaphore_signal(barrier, inc=1, device_id={"ctx": slot(i + 1)}, device_id_type=MESH)

    @functools.partial(each, nseq - 1)
    def _(i):
        pl.semaphore_signal(barrier, inc=1, device_id={"seq": plane(i)}, device_id_type=MESH)

    @functools.partial(each, nctx)
    def _(i):
        fetch(k_hbm, kbuf, k_sem, slot(i)).start()
        fetch(v_hbm, vbuf, v_sem, slot(i)).start()

    rate = rate_in[...]
    rates[ctx] = rate
    lift_out[0:modes, :] = residue_in[...] * jnp.sqrt(minus_expm1(2.0 * rate))
    lift_out[modes:, :] = jnp.broadcast_to(gain_in[...], (lift_out.shape[0] - modes, width))
    lifts[ctx] = lift_out[...]

    pl.semaphore_wait(barrier, nctx + nseq - 2)

    @functools.partial(each, nctx // 2)
    def _(i):
        rate_copy(near(i), ctx).start()

    @functools.partial(each, nctx // 2)
    def _(i):
        lift_copy(near(i), ctx).start()

    @functools.partial(each, nctx)
    def _(i):
        fetch(q_hbm, qbuf, q_sem, slot(i)).start()

    block = lax.broadcasted_iota(jnp.int32, (BLOCKS, LANES), 0)

    def lanes(j):
        return pl.ds(j * LANES if isinstance(j, int) else pl.multiple_of(j * LANES, LANES), LANES)

    def wide(row):
        return jnp.broadcast_to(row, (BLOCKS, LANES))

    def ends(h, first, last):
        @functools.partial(each, last, first=first)
        def _(i):
            c = slot(i)

            if h == 0:
                @pl.when(i > 0)
                def _():
                    rate_copy(c, c).wait_recv()

                    @pl.when(lax.rem(i, 2) == 0)
                    def _():
                        rate_on(c).start()

                fetch(k_hbm, kbuf, k_sem, c).wait()
                fetch(v_hbm, vbuf, v_sem, c).wait()

            @functools.partial(pairs, part)
            def _(n):
                j = h * part + n
                g = c * groups + j
                mixed[g] = (kbuf[c, :, lanes(j)] * vbuf[c, :, lanes(j)]).astype(jnp.float32)
                rate = rates[c, :, lanes(j)]
                pows[g, 0:modes, :] = jnp.exp(-rate)
                pows[g, modes:2 * modes, :] = jnp.exp(-steps * rate)
                p = [wide(pows[g, pl.ds(m, 1), :]) for m in range(modes)]
                state = [mixed[g, pl.ds(0, BLOCKS, stride=steps), :]] * modes
                for a in range(1, steps):
                    x = mixed[g, pl.ds(a, BLOCKS, stride=steps), :]
                    state = [state[m] * p[m] + x for m in range(modes)]
                span = [wide(pows[g, pl.ds(modes + m, 1), :]) for m in range(modes)]
                shift = 1
                while shift < BLOCKS:
                    moved = [pltpu.roll(one, shift, 0) for one in state]
                    state = [
                        state[m] + jnp.where(block >= shift, span[m], 0.0) * moved[m] for m in range(modes)]
                    shift *= 2
                    if shift < BLOCKS:
                        span = [one * one for one in span]
                moved = [pltpu.roll(one, 1, 0) for one in state]
                for m in range(modes):
                    carry[g, m] = jnp.where(block >= 1, moved[m], 0.0)
                    state_out[h, c, pl.ds(m, 1), lanes(n)] = state[m][BLOCKS - 1:, :]

            @pl.when(i > 0)
            def _():
                state_copy(h, c, ctx).start()

    def inside(first, last):
        @functools.partial(each, last, first=first)
        def _(i):
            c = slot(i)

            @pl.when(i > 0)
            def _():
                lift_copy(c, c).wait_recv()

                @pl.when(lax.rem(i, 2) == 0)
                def _():
                    lift_on(c).start()

            @functools.partial(pairs, groups)
            def _(j):
                g = c * groups + j
                p = pows[g, 0:modes, :]
                w = lifts[c, 0:modes, lanes(j)]
                gain = lifts[c, pl.ds(modes, 1), lanes(j)]
                taps = []
                for a in range(steps):
                    tap = jnp.sum(w, axis=0, keepdims=True)
                    taps.append(wide(tap + gain if a == 0 else tap))
                    w = w * p
                    lifted = w if a == 0 else lifted
                y = [taps[a] * mixed[g, pl.ds(0, BLOCKS, stride=steps), :] for a in range(steps)]
                for b in range(1, steps):
                    x = mixed[g, pl.ds(b, BLOCKS, stride=steps), :]
                    for a in range(b, steps):
                        y[a] = y[a] + taps[a - b] * x
                pows[g, modes:2 * modes, :] = lifted
                for a in range(steps):
                    inner[g, a] = y[a]

    def gather_ends(h):
        state_in[h, ctx] = state_out[h, ctx]

        @functools.partial(each, nctx - 1)
        def _(i):
            state_copy(h, slot(i + 1), slot(i + 1)).wait_recv()

        decay = jnp.exp(-tokens * rate_in[:, h * half:(h + 1) * half])

        def link(s, state):
            local_start[h, s] = state
            return state * decay + state_in[h, s]

        totals[h, seq] = lax.fori_loop(0, nctx, link, jnp.zeros_like(decay))

        @functools.partial(each, nseq - 1)
        def _(i):
            total_copy(h, plane(i), seq).start()

    def send_starts(h):
        @functools.partial(each, nseq - 1)
        def _(i):
            total_copy(h, plane(i), plane(i)).wait_recv()

        rate = rate_in[:, h * half:(h + 1) * half]
        span_decay = jnp.exp(-(tokens * nctx) * rate)
        begin = lax.fori_loop(
            0, seq, lambda s, state: state * span_decay + totals[h, s], jnp.zeros_like(rate))

        @functools.partial(each, nctx)
        def _(i):
            c = slot(i)
            reach = jnp.exp(-(tokens * c).astype(jnp.float32) * rate)
            start_out[h, c] = local_start[h, c] + reach * begin

            @pl.when(i > 0)
            def _():
                start_copy(h, c, ctx).start()

        start_in[h, ctx] = start_out[h, ctx]

    far = -steps * block.astype(jnp.float32)

    def outputs(h):
        @functools.partial(each, nctx)
        def _(i):
            c = slot(i)

            @pl.when(i > 0)
            def _():
                start_copy(h, c, c).wait_recv()

            if h == 0:
                fetch(q_hbm, qbuf, q_sem, c).wait()

            @functools.partial(pairs, part)
            def _(n):
                j = h * part + n
                g = c * groups + j
                begin = [
                    jnp.exp(far * wide(rates[c, pl.ds(m, 1), lanes(j)]))
                    * wide(start_in[h, c, pl.ds(m, 1), lanes(n)])
                    for m in range(modes)]
                lifted = [
                    (carry[g, m] + begin[m]) * wide(pows[g, pl.ds(modes + m, 1), :]) for m in range(modes)]
                p = [wide(pows[g, pl.ds(m, 1), :]) for m in range(modes)]
                y = []
                for a in range(steps):
                    terms = [inner[g, a]] + lifted
                    while len(terms) > 1:
                        terms = [sum(terms[n:n + 2][1:], terms[n]) for n in range(0, len(terms), 2)]
                    y += terms
                    if a < steps - 1:
                        lifted = [lifted[m] * p[m] for m in range(modes)]
                for a in range(steps):
                    turned[pl.ds(a, BLOCKS, stride=steps), :] = y[a]
                obuf[c, :, lanes(j)] = qbuf[c, :, lanes(j)] * turned[...].astype(jnp.bfloat16)

            if h == halves - 1:
                store_out(c).start()

    ends(0, 0, nctx)
    if halves == 2:
        ends(1, 0, nctx // 2)
        gather_ends(0)
        ends(1, nctx // 2, nctx)
        inside(0, nctx // 2)
        gather_ends(1)
        send_starts(0)
        inside(nctx // 2, nctx)
        send_starts(1)
        outputs(0)
        outputs(1)
    else:
        inside(0, nctx // 4)
        gather_ends(0)
        inside(nctx // 4, nctx // 2)
        send_starts(0)
        inside(nctx // 2, nctx)
        outputs(0)

    @functools.partial(each, nctx)
    def _(i):
        store_out(slot(i)).wait()

    @functools.partial(each, nctx - 1)
    def _(i):
        c = slot(i + 1)
        for h in range(halves):
            state_copy(h, c, ctx).wait_send()
            start_copy(h, c, ctx).wait_send()

    @functools.partial(each, nctx // 2)
    def _(i):
        rate_copy(near(i), ctx).wait_send()
        lift_copy(near(i), ctx).wait_send()

    @functools.partial(each, nctx // 2, first=1)
    def _(i):
        rate_on(near(i)).wait_send()
        lift_on(near(i)).wait_send()

    @functools.partial(each, nseq - 1)
    def _(i):
        for h in range(halves):
            total_copy(h, plane(i), seq).wait_send()


def local(nctx, nseq, queries, key_proj, value_proj, decay_rate, residue, skip_gain):
    modes, width = decay_rate.shape
    tokens, channels = queries.shape
    groups = channels // LANES
    rows = -(-(modes + 1) // 8) * 8
    f32, bf16 = jnp.float32, jnp.bfloat16
    any_spec = pl.BlockSpec(memory_space=pltpu.HBM)
    piece = pltpu.VMEM((nctx, tokens, width), bf16)
    halves = 2 if (width // LANES) % 2 == 0 else 1
    state = pltpu.VMEM((halves, nctx, modes, width // halves), f32)
    sems = [pltpu.SemaphoreType.DMA((nctx,))] * 8 + [
        pltpu.SemaphoreType.DMA((halves, n)) for n in (nctx, nctx, nseq, nseq, nctx, nctx)] + [
        pltpu.SemaphoreType.DMA((nctx,))] * 2
    return pl.pallas_call(
        functools.partial(kernel, nctx, nseq, modes, halves),
        out_shape=jax.ShapeDtypeStruct((tokens, channels), bf16),
        in_specs=[pl.BlockSpec(memory_space=pltpu.VMEM)] * 3 + [any_spec] * 3,
        out_specs=any_spec,
        scratch_shapes=[
            pltpu.VMEM((nctx, modes, width), f32),
            pltpu.VMEM((nctx, rows, width), f32),
            pltpu.VMEM((rows, width), f32),
            piece, piece, piece, piece,
            pltpu.VMEM((groups, tokens, LANES), f32),
            pltpu.VMEM((groups, tokens // BLOCKS, BLOCKS, LANES), f32),
            pltpu.VMEM((groups, modes, BLOCKS, LANES), f32),
            pltpu.VMEM((groups, 2 * modes, LANES), f32),
            state, state, state,
            pltpu.VMEM((halves, nseq, modes, width // halves), f32),
            state, state,
            pltpu.VMEM((tokens, LANES), f32),
        ] + sems,
        compiler_params=pltpu.CompilerParams(
            collective_id=0, has_side_effects=True, vmem_limit_bytes=60 * 1024 * 1024),
        cost_estimate=pl.CostEstimate(
            flops=tokens * channels * 90, bytes_accessed=8 * tokens * channels,
            transcendentals=groups * modes * LANES * 12),
    )(decay_rate, residue, skip_gain[None], queries, key_proj, value_proj)


def solution(mesh):
    in_specs = (
        P(("seq", "ctx"), None),
        P(("seq", "ctx"), None),
        P(("seq", "ctx"), None),
        P(None, "ctx"),
        P(None, "ctx"),
        P("ctx"),
    )
    body = functools.partial(local, mesh.shape["ctx"], mesh.shape["seq"])
    return jax.shard_map(
        body, mesh=mesh, in_specs=in_specs, out_specs=P(("seq", "ctx"), None), check_vma=False)
```

```python
import functools

import jax
import jax.numpy as jnp
from jax import lax
from jax.experimental import pallas as pl
from jax.experimental.pallas import tpu as pltpu
from jax.sharding import PartitionSpec as P

LANES = 128
BLOCKS = 8
MESH = pl.DeviceIdType.MESH


def minus_expm1(x):
    series = jnp.ones_like(x)
    for n in range(9, 1, -1):
        series = 1.0 - series * x * (1.0 / n)
    return jnp.where(x < 0.25, x * series, 1.0 - jnp.exp(-x))


def kernel(
    nctx, nseq, modes, halves, rate_in, residue_in, gain_in, q_hbm, k_hbm, v_hbm, out_hbm,
    rates, lifts, lift_out, kbuf, vbuf, qbuf, obuf, mixed, inner, carry, pows, state_out, state_in, local_start,
    totals, start_out, start_in, turned,
    k_sem, v_sem, q_sem, o_sem, rate_send, rate_recv, lift_send, lift_recv, st_send, st_recv, tot_send, tot_recv,
    go_send, go_recv, rate_fwd, lift_fwd,
):
    ctx, seq = lax.axis_index("ctx"), lax.axis_index("seq")
    tokens, width = kbuf.shape[1], kbuf.shape[2]
    groups = width // LANES
    steps = tokens // BLOCKS
    part = groups // halves
    half = part * LANES

    bits = [1 << n for n in range(nctx.bit_length() - 1)]
    signs = [b * (1 - 2 * lax.rem(ctx // b, 2)) for b in bits]

    def slot(i):
        place = ctx
        for b, sign in zip(bits, signs):
            place = place + lax.rem(i // b, 2) * sign
        return place

    def columns(c):
        return pl.ds(pl.multiple_of(c * width, LANES), width)

    def fetch(hbm, buf, sem, c):
        return pltpu.make_async_copy(hbm.at[:, columns(c)], buf.at[c], sem.at[c])

    def store_out(c):
        return pltpu.make_async_copy(obuf.at[c], out_hbm.at[:, columns(c)], o_sem.at[c])

    def swap(src, dst, to, send, recv, axis, other):
        return pltpu.make_async_remote_copy(
            src_ref=src, dst_ref=dst.at[to], send_sem=send.at[other], recv_sem=recv.at[to],
            device_id={axis: other}, device_id_type=MESH)

    def rate_copy(c, to):
        return swap(rate_in, rates, to, rate_send, rate_recv, "ctx", c)

    def lift_copy(c, to):
        return swap(lift_out, lifts, to, lift_send, lift_recv, "ctx", c)

    def hand_on(buf, c, send, recv):
        return pltpu.make_async_remote_copy(
            src_ref=buf.at[c], dst_ref=buf.at[c], send_sem=send.at[c], recv_sem=recv.at[c],
            device_id={"ctx": slot(1)}, device_id_type=MESH)

    def rate_on(c):
        return hand_on(rates, c, rate_fwd, rate_recv)

    def lift_on(c):
        return hand_on(lifts, c, lift_fwd, lift_recv)

    def near(i):
        return slot(jnp.where(i == 0, 1, 2 * i))

    def state_copy(h, c, to):
        return swap(state_out.at[h, c], state_in.at[h], to, st_send.at[h], st_recv.at[h], "ctx", c)

    def total_copy(h, s, to):
        return swap(totals.at[h, seq], totals.at[h], to, tot_send.at[h], tot_recv.at[h], "seq", s)

    def start_copy(h, c, to):
        return swap(start_out.at[h, c], start_in.at[h], to, go_send.at[h], go_recv.at[h], "ctx", c)

    def each(count, body, first=0):
        lax.fori_loop(first, count, lambda i, x: (body(i), x)[1], 0)

    def pairs(count, body):
        if count % 2:
            each(count, body)
        elif count == 2:
            for n in range(2):
                body(n)
        else:
            each(count // 2, lambda i: (body(2 * i), body(2 * i + 1)))

    def plane(i):
        return lax.rem(seq + i + 1, nseq)

    barrier = pltpu.get_barrier_semaphore()

    @functools.partial(each, nctx - 1)
    def _(i):
        pl.semaphore_signal(barrier, inc=1, device_id={"ctx": slot(i + 1)}, device_id_type=MESH)

    @functools.partial(each, nseq - 1)
    def _(i):
        pl.semaphore_signal(barrier, inc=1, device_id={"seq": plane(i)}, device_id_type=MESH)

    @functools.partial(each, nctx)
    def _(i):
        fetch(k_hbm, kbuf, k_sem, slot(i)).start()
        fetch(v_hbm, vbuf, v_sem, slot(i)).start()

    rate = rate_in[...]
    rates[ctx] = rate
    lift_out[0:modes, :] = residue_in[...] * jnp.sqrt(minus_expm1(2.0 * rate))
    lift_out[modes:, :] = jnp.broadcast_to(gain_in[...], (lift_out.shape[0] - modes, width))
    lifts[ctx] = lift_out[...]

    pl.semaphore_wait(barrier, nctx + nseq - 2)

    @functools.partial(each, nctx // 2)
    def _(i):
        rate_copy(near(i), ctx).start()

    @functools.partial(each, nctx // 2)
    def _(i):
        lift_copy(near(i), ctx).start()

    @functools.partial(each, nctx)
    def _(i):
        fetch(q_hbm, qbuf, q_sem, slot(i)).start()

    block = lax.broadcasted_iota(jnp.int32, (BLOCKS, LANES), 0)

    def lanes(j):
        return pl.ds(j * LANES if isinstance(j, int) else pl.multiple_of(j * LANES, LANES), LANES)

    def wide(row):
        return jnp.broadcast_to(row, (BLOCKS, LANES))

    def ends(h, first, last):
        @functools.partial(each, last, first=first)
        def _(i):
            c = slot(i)

            if h == 0:
                @pl.when(i > 0)
                def _():
                    rate_copy(c, c).wait_recv()

                    @pl.when(lax.rem(i, 2) == 0)
                    def _():
                        rate_on(c).start()

                fetch(k_hbm, kbuf, k_sem, c).wait()
                fetch(v_hbm, vbuf, v_sem, c).wait()

            @functools.partial(pairs, part)
            def _(n):
                j = h * part + n
                g = c * groups + j
                mixed[g] = (kbuf[c, :, lanes(j)] * vbuf[c, :, lanes(j)]).astype(jnp.float32)
                rate = rates[c, :, lanes(j)]
                pows[g, 0:modes, :] = jnp.exp(-rate)
                pows[g, modes:2 * modes, :] = jnp.exp(-steps * rate)
                p = [wide(pows[g, pl.ds(m, 1), :]) for m in range(modes)]
                state = [mixed[g, pl.ds(0, BLOCKS, stride=steps), :]] * modes
                for a in range(1, steps):
                    x = mixed[g, pl.ds(a, BLOCKS, stride=steps), :]
                    state = [state[m] * p[m] + x for m in range(modes)]
                span = [wide(pows[g, pl.ds(modes + m, 1), :]) for m in range(modes)]
                shift = 1
                while shift < BLOCKS:
                    moved = [pltpu.roll(one, shift, 0) for one in state]
                    state = [
                        state[m] + jnp.where(block >= shift, span[m], 0.0) * moved[m] for m in range(modes)]
                    shift *= 2
                    if shift < BLOCKS:
                        span = [one * one for one in span]
                moved = [pltpu.roll(one, 1, 0) for one in state]
                for m in range(modes):
                    carry[g, m] = jnp.where(block >= 1, moved[m], 0.0)
                    state_out[h, c, pl.ds(m, 1), lanes(n)] = state[m][BLOCKS - 1:, :]

            @pl.when(i > 0)
            def _():
                state_copy(h, c, ctx).start()

    def inside(first, last):
        @functools.partial(each, last, first=first)
        def _(i):
            c = slot(i)

            @pl.when(i > 0)
            def _():
                lift_copy(c, c).wait_recv()

                @pl.when(lax.rem(i, 2) == 0)
                def _():
                    lift_on(c).start()

            @functools.partial(pairs, groups)
            def _(j):
                g = c * groups + j
                p = pows[g, 0:modes, :]
                w = lifts[c, 0:modes, lanes(j)]
                gain = lifts[c, pl.ds(modes, 1), lanes(j)]
                taps = []
                for a in range(steps):
                    tap = sum(w[n:n + BLOCKS] for n in range(0, modes, BLOCKS))
                    shift = BLOCKS // 2
                    while shift:
                        tap = tap + pltpu.roll(tap, shift, 0)
                        shift //= 2
                    taps.append(tap + wide(gain) if a == 0 else tap)
                    w = w * p
                    lifted = w if a == 0 else lifted
                y = [taps[a] * mixed[g, pl.ds(0, BLOCKS, stride=steps), :] for a in range(steps)]
                for b in range(1, steps):
                    x = mixed[g, pl.ds(b, BLOCKS, stride=steps), :]
                    for a in range(b, steps):
                        y[a] = y[a] + taps[a - b] * x
                pows[g, modes:2 * modes, :] = lifted
                for a in range(steps):
                    inner[g, a] = y[a]

    def gather_ends(h):
        state_in[h, ctx] = state_out[h, ctx]

        @functools.partial(each, nctx - 1)
        def _(i):
            state_copy(h, slot(i + 1), slot(i + 1)).wait_recv()

        decay = jnp.exp(-tokens * rate_in[:, h * half:(h + 1) * half])

        def link(s, state):
            local_start[h, s] = state
            return state * decay + state_in[h, s]

        totals[h, seq] = lax.fori_loop(0, nctx, link, jnp.zeros_like(decay))

        @functools.partial(each, nseq - 1)
        def _(i):
            total_copy(h, plane(i), seq).start()

    def send_starts(h):
        @functools.partial(each, nseq - 1)
        def _(i):
            total_copy(h, plane(i), plane(i)).wait_recv()

        rate = rate_in[:, h * half:(h + 1) * half]
        span_decay = jnp.exp(-(tokens * nctx) * rate)
        begin = lax.fori_loop(
            0, seq, lambda s, state: state * span_decay + totals[h, s], jnp.zeros_like(rate))

        @functools.partial(each, nctx)
        def _(i):
            c = slot(i)
            reach = jnp.exp(-(tokens * c).astype(jnp.float32) * rate)
            start_out[h, c] = local_start[h, c] + reach * begin

            @pl.when(i > 0)
            def _():
                start_copy(h, c, ctx).start()

        start_in[h, ctx] = start_out[h, ctx]

    far = -steps * block.astype(jnp.float32)

    def outputs(h):
        @functools.partial(each, nctx)
        def _(i):
            c = slot(i)

            @pl.when(i > 0)
            def _():
                start_copy(h, c, c).wait_recv()

            if h == 0:
                fetch(q_hbm, qbuf, q_sem, c).wait()

            @functools.partial(pairs, part)
            def _(n):
                j = h * part + n
                g = c * groups + j
                begin = [
                    jnp.exp(far * wide(rates[c, pl.ds(m, 1), lanes(j)]))
                    * wide(start_in[h, c, pl.ds(m, 1), lanes(n)])
                    for m in range(modes)]
                lifted = [
                    (carry[g, m] + begin[m]) * wide(pows[g, pl.ds(modes + m, 1), :]) for m in range(modes)]
                p = [wide(pows[g, pl.ds(m, 1), :]) for m in range(modes)]
                y = []
                for a in range(steps):
                    terms = [inner[g, a]] + lifted
                    while len(terms) > 1:
                        terms = [sum(terms[n:n + 2][1:], terms[n]) for n in range(0, len(terms), 2)]
                    y += terms
                    if a < steps - 1:
                        lifted = [lifted[m] * p[m] for m in range(modes)]
                for a in range(steps):
                    turned[pl.ds(a, BLOCKS, stride=steps), :] = y[a]
                obuf[c, :, lanes(j)] = qbuf[c, :, lanes(j)] * turned[...].astype(jnp.bfloat16)

            if h == halves - 1:
                store_out(c).start()

    ends(0, 0, nctx)
    if halves == 2:
        ends(1, 0, nctx // 2)
        gather_ends(0)
        ends(1, nctx // 2, nctx)
        inside(0, nctx // 2)
        gather_ends(1)
        send_starts(0)
        inside(nctx // 2, nctx)
        send_starts(1)
        outputs(0)
        outputs(1)
    else:
        inside(0, nctx // 4)
        gather_ends(0)
        inside(nctx // 4, nctx // 2)
        send_starts(0)
        inside(nctx // 2, nctx)
        outputs(0)

    @functools.partial(each, nctx)
    def _(i):
        store_out(slot(i)).wait()

    @functools.partial(each, nctx - 1)
    def _(i):
        c = slot(i + 1)
        for h in range(halves):
            state_copy(h, c, ctx).wait_send()
            start_copy(h, c, ctx).wait_send()

    @functools.partial(each, nctx // 2)
    def _(i):
        rate_copy(near(i), ctx).wait_send()
        lift_copy(near(i), ctx).wait_send()

    @functools.partial(each, nctx // 2, first=1)
    def _(i):
        rate_on(near(i)).wait_send()
        lift_on(near(i)).wait_send()

    @functools.partial(each, nseq - 1)
    def _(i):
        for h in range(halves):
            total_copy(h, plane(i), seq).wait_send()


def local(nctx, nseq, queries, key_proj, value_proj, decay_rate, residue, skip_gain):
    modes, width = decay_rate.shape
    tokens, channels = queries.shape
    groups = channels // LANES
    rows = -(-(modes + 1) // 8) * 8
    f32, bf16 = jnp.float32, jnp.bfloat16
    any_spec = pl.BlockSpec(memory_space=pltpu.HBM)
    piece = pltpu.VMEM((nctx, tokens, width), bf16)
    halves = 2 if (width // LANES) % 2 == 0 else 1
    state = pltpu.VMEM((halves, nctx, modes, width // halves), f32)
    sems = [pltpu.SemaphoreType.DMA((nctx,))] * 8 + [
        pltpu.SemaphoreType.DMA((halves, n)) for n in (nctx, nctx, nseq, nseq, nctx, nctx)] + [
        pltpu.SemaphoreType.DMA((nctx,))] * 2
    return pl.pallas_call(
        functools.partial(kernel, nctx, nseq, modes, halves),
        out_shape=jax.ShapeDtypeStruct((tokens, channels), bf16),
        in_specs=[pl.BlockSpec(memory_space=pltpu.VMEM)] * 3 + [any_spec] * 3,
        out_specs=any_spec,
        scratch_shapes=[
            pltpu.VMEM((nctx, modes, width), f32),
            pltpu.VMEM((nctx, rows, width), f32),
            pltpu.VMEM((rows, width), f32),
            piece, piece, piece, piece,
            pltpu.VMEM((groups, tokens, LANES), f32),
            pltpu.VMEM((groups, tokens // BLOCKS, BLOCKS, LANES), f32),
            pltpu.VMEM((groups, modes, BLOCKS, LANES), f32),
            pltpu.VMEM((groups, 2 * modes, LANES), f32),
            state, state, state,
            pltpu.VMEM((halves, nseq, modes, width // halves), f32),
            state, state,
            pltpu.VMEM((tokens, LANES), f32),
        ] + sems,
        compiler_params=pltpu.CompilerParams(
            collective_id=0, has_side_effects=True, vmem_limit_bytes=60 * 1024 * 1024),
        cost_estimate=pl.CostEstimate(
            flops=tokens * channels * 90, bytes_accessed=8 * tokens * channels,
            transcendentals=groups * modes * LANES * 12),
    )(decay_rate, residue, skip_gain[None], queries, key_proj, value_proj)


def solution(mesh):
    in_specs = (
        P(("seq", "ctx"), None),
        P(("seq", "ctx"), None),
        P(("seq", "ctx"), None),
        P(None, "ctx"),
        P(None, "ctx"),
        P("ctx"),
    )
    body = functools.partial(local, mesh.shape["ctx"], mesh.shape["seq"])
    return jax.shard_map(
        body, mesh=mesh, in_specs=in_specs, out_specs=P(("seq", "ctx"), None), check_vma=False)
```
